32 devices in a mesh: tm: 4 (over z), space: 8 (over y, x, core).
Axes of the slice: x: 2, y: 2, z: 4, core: 2. Of those that a mesh axis runs over, the one named last changes fastest.
Arguments:
- forward_states: bfloat16 [16, 4, 32, 8, 128], P('tm', None, 'space'), may hold values from -3 to 3
- adjoint_source: float32 [16, 4, 32, 8, 128], P('tm', None, 'space'), may hold values from -6 to 6
- source_gain: float32 [4, 32, 8, 128], P(None, 'space'), may hold values from -4 to 0.3
- guess_pairs: float32 [4, 2, 4, 32, 8, 128], P('tm', None, None, 'space'), may hold values from -6 to 6
Outputs:
- corrected: float32 [4, 2, 4, 32, 8, 128], P('tm', None, None, 'space')
- gradient: float32 [4, 32, 8, 128], P(None, 'space')
The draws below stay inside these ranges and needn't reach their ends.
All inputs are finite; a program needn't handle non-finite values.
Results may differ from the reference program's by a relative error of at most 0.0003.
Values sent between devices are 32-bit elements; how exact they have to be, the bound alone decides.
A program may use at most 64 MiB of HBM per device.

```python
import jax
import jax.numpy as jnp
from jax import lax

FIELDS = 4
CY = 8
CZ = 128
COARSEN = 4
SWEEPS = 4
STEPS = 16
NX = 32
N_TM = 4


def steps_of(own_key, shape, pieces, low, top_value):
    def one(dim, parts):
        heights = jax.random.uniform(jax.random.fold_in(jax.random.fold_in(own_key, 6), dim), (parts,), jnp.float32, low / len(pieces), top_value / len(pieces))
        return jnp.repeat(jnp.exp(heights), shape[dim] // parts).reshape((-1,) + (1,) * (len(shape) - dim - 1))

    level = one(*pieces[0])
    for cut in pieces[1:]:
        level = level * one(*cut)
    return level


def bell_draw(key, shape, scale, limit, pieces=(), dtype=jnp.bfloat16):
    factor_of = steps_of(key, shape, pieces, -0.22, 0.18) if pieces else 1.0
    values = jax.random.normal(key, shape, jnp.float32) * scale * factor_of
    return jnp.minimum(jnp.maximum(values, -limit), limit).astype(dtype)


def setup_inputs(seed: int = 0) -> dict:
    seeds = jax.random.split(jax.random.key(seed), 5)
    forward_states = bell_draw(seeds[0], (STEPS, FIELDS, NX, CY, CZ), 0.8, 3.0, ((0, 4), (2, 8)))
    adjoint_source = bell_draw(seeds[1], (STEPS, FIELDS, NX, CY, CZ), 1.0, 6.0, ((0, 4), (2, 8)), jnp.float32)
    source_gain = jnp.clip(-4.0 + 4.3 * jax.random.uniform(seeds[2], (FIELDS, NX, CY, CZ), jnp.float32) ** steps_of(seeds[2], (FIELDS, NX, CY, CZ), ((1, 8),), -0.2, 0.2), -4.0, 0.3)
    guess_pairs = bell_draw(seeds[3], (N_TM, 2, FIELDS, NX, CY, CZ), 1.0, 6.0, ((0, 4), (3, 8)), jnp.float32)
    return {"forward_states": forward_states, "adjoint_source": adjoint_source, "source_gain": source_gain, "guess_pairs": guess_pairs}


diffusion = (2.4, 1.2, 0.6, 4.0)
fibre_weight = 128.0
reaction = ((-14.4, 7.2, -4.8, 2.4), (4.8, -19.2, 7.2, -4.8), (-7.2, 2.4, -12.0, 7.2), (4.8, -7.2, 2.4, -38.4))
self_rates = (-14.4, -19.2, -12.0, -38.4)
masses = (1.0, 1.0, 1.0, 0.0)
fine_rate = 3.0
coarse_rate = 0.75
time_step = 0.5
operator_scale = 0.0078125
state_weight = 0.1
gain_weight = 0.25


def column(values):
    return jnp.array(values, jnp.float32).reshape(4, 1, 1, 1)


def from_below(field, axis):
    extent = field.shape[axis]
    retained = lax.slice_in_dim(field, 0, extent - 1, axis=axis)
    widths = [(0, 0)] * field.ndim
    widths[axis] = (1, 0)
    return jnp.pad(retained, widths)


def from_above(field, axis):
    extent = field.shape[axis]
    retained = lax.slice_in_dim(field, 1, extent, axis=axis)
    widths = [(0, 0)] * field.ndim
    widths[axis] = (0, 1)
    return jnp.pad(retained, widths)


def neighbours(field):
    running = fibre_weight * (from_below(field, 1) + from_above(field, 1))
    running = running + from_below(field, 2) + from_above(field, 2)
    return running + from_below(field, 3) + from_above(field, 3)


def coupling(field):
    stacked_rows = []
    for target in range(4):
        running = jnp.zeros_like(field[0])
        for source in range(4):
            if source != target:
                running = running + reaction[source][target] * field[source]
        stacked_rows.append(running)
    return jnp.stack(stacked_rows)


def jacobi_sweep(field, right_side, diagonal):
    spread = column(diffusion) * neighbours(field) + coupling(field)
    return (right_side + operator_scale * spread) / diagonal


def make_diagonal(state, source_gain, rate):
    stencil_total = (2.0 * fibre_weight + 4.0) * column(diffusion)
    spatial = operator_scale * (stencil_total - column(self_rates))
    return rate * column(masses) + spatial + state_weight * state * state - gain_weight * source_gain


def implicit_solve(right_side, diagonal):
    iterate = right_side / diagonal
    for sweep_count in range(SWEEPS):
        iterate = jacobi_sweep(iterate, right_side, diagonal)
    return iterate


def coarse_step(pair, diagonal):
    solved = implicit_solve(column(masses) * (pair[0] - 0.25 * pair[1]), diagonal)
    return jnp.stack([solved, 0.5 * (solved + pair[0])])


def reference(forward_states, adjoint_source, source_gain, guess_pairs):
    states = forward_states.astype(jnp.float32)
    mass = column(masses)
    zero_pair = jnp.zeros_like(guess_pairs[0])
    adjoints = [None] * (COARSEN * N_TM)
    relaxed = []
    for interval in range(N_TM):
        later = guess_pairs[interval + 1] if interval + 1 < N_TM else zero_pair
        ahead_one, ahead_two = later[0], later[1]
        for offset in range(COARSEN - 1, -1, -1):
            position = interval * COARSEN + offset
            diagonal = make_diagonal(states[position], source_gain, fine_rate)
            right_side = adjoint_source[position] + mass * (4.0 * ahead_one - ahead_two)
            current = implicit_solve(right_side, diagonal)
            adjoints[position] = current
            ahead_two, ahead_one = ahead_one, current
        relaxed.append(jnp.stack([adjoints[interval * COARSEN], adjoints[interval * COARSEN + 1]]))
    running = adjoints[0] * states[0]
    for position in range(1, COARSEN * N_TM):
        running = running + adjoints[position] * states[position]
    gradient = time_step * running
    coarse_diags = [make_diagonal(states[interval * COARSEN], source_gain, coarse_rate) for interval in range(N_TM)]
    offsets = []
    for interval in range(N_TM):
        following = relaxed[interval + 1] if interval + 1 < N_TM else zero_pair
        offsets.append(relaxed[interval] - coarse_step(following, coarse_diags[interval]))
    results = [None] * N_TM
    carried = zero_pair
    for interval in range(N_TM - 1, -1, -1):
        carried = coarse_step(carried, coarse_diags[interval]) + offsets[interval]
        results[interval] = carried
    return jnp.stack(results), gradient
```

```python
import functools

import jax
import jax.numpy as jnp
from jax import lax
from jax.experimental import pallas as pl
from jax.experimental.pallas import tpu as pltpu
from jax.sharding import PartitionSpec as P

SWEEPS = 4
FIELDS = 4
MASSIVE = 3

diffusion = (2.4, 1.2, 0.6, 4.0)
fibre_weight = 128.0
reaction = (
    (-14.4, 7.2, -4.8, 2.4),
    (4.8, -19.2, 7.2, -4.8),
    (-7.2, 2.4, -12.0, 7.2),
    (4.8, -7.2, 2.4, -38.4),
)
self_rates = (-14.4, -19.2, -12.0, -38.4)
masses = (1.0, 1.0, 1.0, 0.0)
fine_rate = 3.0
coarse_rate = 0.75
time_step = 0.5
operator_scale = 0.0078125
state_weight = 0.1
gain_weight = 0.25

MESH = pl.DeviceIdType.MESH


def kernel(
    steps, thick, tms, spaces,
    states_ref, source_ref, gain_ref, guess_ref,
    corrected_ref, gradient_ref,
    inv, right, rel_right, cor_right, xa, xb, adj, zero_q, rel_q, cor_q, offs, cor,
    w_src, w_got, g_src, g_got, rel_src, rel_p0, cor_src, cor_p0,
    part, part_got, whole,
    halo_send, halo_recv, z_send, z_recv, grad_send, grad_recv,
):
    t = lax.axis_index("tm")
    s = lax.axis_index("space")
    has_up, has_dn = s < spaces - 1, s > 0
    has_next, has_prev = t < tms - 1, t > 0
    wide = thick + 2 * SWEEPS
    own = pl.ds(SWEEPS, thick)
    low = pl.ds(0, SWEEPS)
    high = pl.ds(SWEEPS + thick, SWEEPS)
    coarse = steps
    row = lax.broadcasted_iota(jnp.int32, (8, 128), 0)
    col = lax.broadcasted_iota(jnp.int32, (8, 128), 1)

    def halo_copies(index, view):
        up = pltpu.make_async_remote_copy(
            view(own), view(low), halo_send.at[index, 0], halo_recv.at[index, 0],
            device_id={"space": s + 1}, device_id_type=MESH,
        )
        dn = pltpu.make_async_remote_copy(
            view(own), view(high), halo_send.at[index, 1], halo_recv.at[index, 1],
            device_id={"space": s - 1}, device_id_type=MESH,
        )
        return up, dn

    def halo_start(copies):
        pl.when(has_up)(copies[0].start)
        pl.when(has_dn)(copies[1].start)

    def halo_wait(copies):
        pl.when(has_dn)(copies[0].wait_recv)
        pl.when(has_up)(copies[1].wait_recv)

    def halo_sent(copies):
        pl.when(has_up)(copies[0].wait_send)
        pl.when(has_dn)(copies[1].wait_send)

    def to_previous(index, src, dst):
        return pltpu.make_async_remote_copy(
            src, dst, z_send.at[index], z_recv.at[index],
            device_id={"tm": t - 1}, device_id_type=MESH,
        )

    inv_copies = [
        halo_copies(n, lambda p, n=n: inv.at[n, :, p]) for n in range(steps + 1)
    ]
    last = steps - 1
    right_copies = [
        halo_copies(
            steps + 1 + n,
            (lambda p, n=n: right.at[n, :, p])
            if n == last
            else (lambda p, n=n: right.at[n, pl.ds(0, MASSIVE), p]),
        )
        for n in range(steps)
    ]
    rest_copies = halo_copies(
        2 * steps + 1, lambda p: right.at[pl.ds(0, last), MASSIVE, p]
    )
    rel_copies = halo_copies(
        2 * steps + 2, lambda p: rel_right.at[pl.ds(0, MASSIVE), p]
    )
    cor_copies = halo_copies(
        2 * steps + 3, lambda p: cor_right.at[pl.ds(0, MASSIVE), p]
    )
    z_w = to_previous(0, w_src, w_got)
    z_g = to_previous(1, g_src, g_got)
    z_rel = to_previous(2, rel_src, rel_right.at[pl.ds(0, MASSIVE), own])
    z_rel_p0 = to_previous(3, adj.at[0], rel_p0)
    z_cor = to_previous(4, cor_src, cor_right.at[pl.ds(0, MASSIVE), own])
    z_cor_p0 = to_previous(5, cor.at[0], cor_p0)

    rel_right[...] = jnp.zeros_like(rel_right)
    cor_right[...] = jnp.zeros_like(cor_right)

    def clear(span):
        inv[:, :, span] = jnp.zeros((steps + 1, FIELDS, SWEEPS, 8, 128), jnp.float32)
        right[:, :, span] = jnp.zeros((steps, FIELDS, SWEEPS, 8, 128), jnp.float32)

    @pl.when(s == 0)
    def _():
        clear(low)

    @pl.when(s == spaces - 1)
    def _():
        clear(high)

    @pl.when(t == tms - 1)
    def _():
        w_got[...] = jnp.zeros_like(w_got)
        g_got[...] = jnp.zeros_like(g_got)

    barrier = pltpu.get_barrier_semaphore()
    for hop in range(1, tms):
        pl.semaphore_signal(
            barrier, inc=1, device_id={"tm": lax.rem(t + hop, tms)}, device_id_type=MESH
        )

    @pl.when(has_up)
    def _():
        pl.semaphore_signal(barrier, inc=1, device_id={"space": s + 1}, device_id_type=MESH)

    @pl.when(has_dn)
    def _():
        pl.semaphore_signal(barrier, inc=1, device_id={"space": s - 1}, device_id_type=MESH)

    def fill_inverse(slot, n, rate):
        for i in range(FIELDS):
            u = states_ref[n, i].astype(jnp.float32)
            base = rate * masses[i] + operator_scale * (
                (2.0 * fibre_weight + 4.0) * diffusion[i] - self_rates[i]
            )
            diagonal = base + state_weight * u * u - gain_weight * gain_ref[i]
            inv[slot, i, own] = 1.0 / diagonal

    for i in range(MASSIVE):
        w_src[i] = 4.0 * guess_ref[0, 0, i] - guess_ref[0, 1, i]
        g_src[i] = guess_ref[0, 0, i]
    fill_inverse(last, last, fine_rate)

    pl.semaphore_wait(
        barrier, tms - 1 + has_up.astype(jnp.int32) + has_dn.astype(jnp.int32)
    )

    @pl.when(has_prev)
    def _():
        z_w.start()
        z_g.start()

    halo_start(inv_copies[last])
    for n in range(last):
        fill_inverse(n, n, fine_rate)
    fill_inverse(coarse, 0, coarse_rate)
    for n in range(steps):
        right[n, MASSIVE, own] = source_ref[n, MASSIVE]
    pl.when(has_next)(z_w.wait_recv)
    for i in range(MASSIVE):
        right[last, i, own] = source_ref[last, i] + w_got[i]
    halo_start(right_copies[last])
    halo_start(rest_copies)
    for n in range(last - 1, -1, -1):
        halo_start(inv_copies[n])
    halo_start(inv_copies[coarse])

    def sweep(src, dst, rhs, factor, edge, shift):
        def body(p, carry):
            x = [src[i, p] for i in range(FIELDS)]
            for i in range(FIELDS):
                vertical = src[i, p - 1] + src[i, p + 1]
                sides = (
                    jnp.where(row > 0, pltpu.roll(x[i], 1, 0), 0.0)
                    + jnp.where(row < 7, pltpu.roll(x[i], 7, 0), 0.0)
                    + jnp.where(col > 0, pltpu.roll(x[i], 1, 1), 0.0)
                    + jnp.where(col < 127, pltpu.roll(x[i], 127, 1), 0.0)
                )
                total = rhs[i, p] + (operator_scale * fibre_weight * diffusion[i]) * vertical
                total = total + (operator_scale * diffusion[i]) * sides
                for j in range(FIELDS):
                    if j != i:
                        total = total + (operator_scale * reaction[j][i]) * x[j]
                dst[i, p - shift] = total * factor[i, p]
            return carry

        lax.fori_loop(edge, wide - edge, body, 0, unroll=True)

    def solve(rhs, factor, result):
        def begin(p, carry):
            for i in range(FIELDS):
                xa[i, p] = rhs[i, p] * factor[i, p]
            return carry

        lax.fori_loop(0, wide, begin, 0, unroll=True)
        sweep(xa, xb, rhs, factor, 1, 0)
        sweep(xb, xa, rhs, factor, 2, 0)
        sweep(xa, xb, rhs, factor, 3, 0)
        sweep(xb, result, rhs, factor, 4, SWEEPS)

    for n in range(last, -1, -1):
        halo_wait(inv_copies[n])
        halo_wait(right_copies[n])
        if n == last - 1:
            halo_wait(rest_copies)
        solve(right.at[n], inv.at[n], adj.at[n])
        if n == last:
            pl.when(has_next)(z_g.wait_recv)
        if n > 0:
            for i in range(MASSIVE):
                before = g_got[i] if n == last else adj[n + 1, i]
                right[n - 1, i, own] = source_ref[n - 1, i] + (4.0 * adj[n, i] - before)
            halo_start(right_copies[n - 1])
        if n == 1:
            halo_wait(inv_copies[coarse])

            @pl.when(t == tms - 1)
            def _():
                solve(rel_right, inv.at[coarse], zero_q)

        if n == 0:
            for i in range(MASSIVE):
                rel_src[i] = adj[0, i] - 0.25 * adj[1, i]

            @pl.when(has_prev)
            def _():
                z_rel.start()
                z_rel_p0.start()

        for i in range(FIELDS):
            term = adj[n, i] * states_ref[n, i].astype(jnp.float32)
            spot = pl.ds(i * thick, thick)
            part[spot] = term if n == last else part[spot] + term

    def send_corrected():
        for i in range(MASSIVE):
            cor_src[i] = cor[0, i] - 0.25 * cor[1, i]

        @pl.when(has_prev)
        def _():
            z_cor.start()
            z_cor_p0.start()

    @pl.when(t == tms - 1)
    def _():
        for i in range(FIELDS):
            zero_p1 = 0.5 * (zero_q[i] + 0.0)
            cor[0, i] = zero_q[i] + (adj[0, i] - zero_q[i])
            cor[1, i] = zero_p1 + (adj[1, i] - zero_p1)
        send_corrected()

    chunk = FIELDS * thick // tms
    grad_one, grad_two, grad_in = [], [], []
    for hop in range(1, tms):
        target = lax.rem(t + hop, tms)
        origin = lax.rem(t + tms - hop, tms)
        grad_one.append(
            pltpu.make_async_remote_copy(
                part.at[pl.ds(target * chunk, chunk)], part_got.at[hop - 1],
                grad_send.at[0, hop - 1], grad_recv.at[0, hop - 1],
                device_id={"tm": target}, device_id_type=MESH,
            )
        )
        mine = whole.at[pl.ds(t * chunk, chunk)]
        grad_two.append(
            pltpu.make_async_remote_copy(
                mine, mine, grad_send.at[1, hop - 1], grad_recv.at[1, hop - 1],
                device_id={"tm": target}, device_id_type=MESH,
            )
        )
        theirs = whole.at[pl.ds(origin * chunk, chunk)]
        grad_in.append(
            pltpu.make_async_remote_copy(
                theirs, theirs, grad_send.at[1, hop - 1], grad_recv.at[1, hop - 1],
                device_id={"tm": target}, device_id_type=MESH,
            )
        )
    for copy in grad_one:
        copy.start()

    def take_corrected():
        z_cor.wait_recv()
        halo_start(cor_copies)

    @pl.when(has_next)
    def _():
        z_rel.wait_recv()
        halo_start(rel_copies)

        @pl.when(t == tms - 2)
        def _():
            take_corrected()

        halo_wait(rel_copies)
        solve(rel_right, inv.at[coarse], rel_q)
        z_rel_p0.wait_recv()
        for i in range(FIELDS):
            offs[0, i] = adj[0, i] - rel_q[i]
            offs[1, i] = adj[1, i] - 0.5 * (rel_q[i] + rel_p0[i])

    for copy in grad_one:
        copy.wait_recv()
    total = part[pl.ds(t * chunk, chunk)]
    for hop in range(1, tms):
        total = total + part_got[hop - 1]
    whole[pl.ds(t * chunk, chunk)] = time_step * total
    for copy in grad_two:
        copy.start()

    @pl.when(has_next)
    def _():
        @pl.when(t < tms - 2)
        def _():
            take_corrected()

        halo_wait(cor_copies)
        solve(cor_right, inv.at[coarse], cor_q)
        z_cor_p0.wait_recv()
        for i in range(FIELDS):
            cor[0, i] = cor_q[i] + offs[0, i]
            cor[1, i] = 0.5 * (cor_q[i] + cor_p0[i]) + offs[1, i]
        send_corrected()

    for pair in range(2):
        corrected_ref[0, pair] = cor[pair]
    for copy in grad_in:
        copy.wait_recv()
    for i in range(FIELDS):
        gradient_ref[i] = whole[pl.ds(i * thick, thick)]

    for copies in inv_copies + right_copies + [rest_copies]:
        halo_sent(copies)

    @pl.when(has_next)
    def _():
        halo_sent(rel_copies)
        halo_sent(cor_copies)

    @pl.when(has_prev)
    def _():
        for copy in (z_w, z_g, z_rel, z_rel_p0, z_cor, z_cor_p0):
            copy.wait_send()

    for copy in grad_one + grad_two:
        copy.wait_send()


def on_device(tms, spaces, forward_states, adjoint_source, source_gain, guess_pairs):
    steps, _, thick = forward_states.shape[:3]
    wide = thick + 2 * SWEEPS
    vmem = lambda *shape: pltpu.VMEM(shape + (8, 128), jnp.float32)
    chunk = FIELDS * thick // tms
    in_vmem = pl.BlockSpec(memory_space=pltpu.VMEM)
    return pl.pallas_call(
        functools.partial(kernel, steps, thick, tms, spaces),
        out_shape=(
            jax.ShapeDtypeStruct(guess_pairs.shape, jnp.float32),
            jax.ShapeDtypeStruct(source_gain.shape, jnp.float32),
        ),
        in_specs=[in_vmem] * 4,
        out_specs=(in_vmem, in_vmem),
        scratch_shapes=[
            vmem(steps + 1, FIELDS, wide),
            vmem(steps, FIELDS, wide),
            vmem(FIELDS, wide),
            vmem(FIELDS, wide),
            vmem(FIELDS, wide),
            vmem(FIELDS, wide),
            vmem(steps, FIELDS, thick),
            vmem(FIELDS, thick),
            vmem(FIELDS, thick),
            vmem(FIELDS, thick),
            vmem(2, FIELDS, thick),
            vmem(2, FIELDS, thick),
            vmem(MASSIVE, thick),
            vmem(MASSIVE, thick),
            vmem(MASSIVE, thick),
            vmem(MASSIVE, thick),
            vmem(MASSIVE, thick),
            vmem(FIELDS, thick),
            vmem(MASSIVE, thick),
            vmem(FIELDS, thick),
            vmem(FIELDS * thick),
            vmem(tms - 1, chunk),
            vmem(FIELDS * thick),
            pltpu.SemaphoreType.DMA((2 * steps + 4, 2)),
            pltpu.SemaphoreType.DMA((2 * steps + 4, 2)),
            pltpu.SemaphoreType.DMA((6,)),
            pltpu.SemaphoreType.DMA((6,)),
            pltpu.SemaphoreType.DMA((2, tms - 1)),
            pltpu.SemaphoreType.DMA((2, tms - 1)),
        ],
        compiler_params=pltpu.CompilerParams(
            collective_id=0, has_side_effects=True, vmem_limit_bytes=32 * 1024 * 1024
        ),
        name="adjoint_cycle",
    )(forward_states, adjoint_source, source_gain, guess_pairs)


def solution(mesh):
    placed = (
        P("tm", None, "space", None, None),
        P("tm", None, "space", None, None),
        P(None, "space", None, None),
        P("tm", None, None, "space", None, None),
    )
    return jax.shard_map(
        functools.partial(on_device, mesh.shape["tm"], mesh.shape["space"]),
        mesh=mesh,
        in_specs=placed,
        out_specs=(P("tm", None, None, "space", None, None), P(None, "space", None, None)),
        check_vma=False,
    )
```

```python
import functools

import jax
import jax.numpy as jnp
from jax import lax
from jax.experimental import pallas as pl
from jax.experimental.pallas import tpu as pltpu
from jax.sharding import PartitionSpec as P

SWEEPS = 4
FIELDS = 4
MASSIVE = 3

diffusion = (2.4, 1.2, 0.6, 4.0)
fibre_weight = 128.0
reaction = (
    (-14.4, 7.2, -4.8, 2.4),
    (4.8, -19.2, 7.2, -4.8),
    (-7.2, 2.4, -12.0, 7.2),
    (4.8, -7.2, 2.4, -38.4),
)
self_rates = (-14.4, -19.2, -12.0, -38.4)
masses = (1.0, 1.0, 1.0, 0.0)
fine_rate = 3.0
coarse_rate = 0.75
time_step = 0.5
operator_scale = 0.0078125
state_weight = 0.1
gain_weight = 0.25

MESH = pl.DeviceIdType.MESH


def kernel(
    steps, thick, tms, spaces,
    states_hbm, source_hbm, gain_hbm, guess_hbm,
    corrected_ref, gradient_ref,
    states_ref, source_ref, gain_ref, guess_ref,
    inv, inv_turned, right, right_turned, w_right, rel_right, cor_right, xs,
    adj, zero_q, rel_q, cor_q, offs, cor,
    w_src, w_turned, g_src, g_got, rel_src, rel_turned, rel_p0, cor_src, cor_turned, cor_p0,
    passed_on, part, part_got, whole,
    load_sem, halo_send, halo_recv, z_send, z_recv, grad_send, grad_recv,
):
    t = lax.axis_index("tm")
    s = lax.axis_index("space")
    odd = lax.rem(s, 2)
    sibling = s + 1 - 2 * odd
    other = s - 1 + 2 * odd
    has_other = jnp.logical_and(other >= 0, other < spaces)
    has_next, has_prev = t < tms - 1, t > 0
    wide = thick + 2 * SWEEPS
    first, end = SWEEPS, SWEEPS + thick
    own = pl.ds(SWEEPS, thick)
    low = pl.ds(0, SWEEPS)
    high = pl.ds(SWEEPS + thick, SWEEPS)
    heavy = pl.ds(0, MASSIVE)
    coarse = steps
    last = steps - 1
    row = lax.broadcasted_iota(jnp.int32, (8, 128), 0)
    col = lax.broadcasted_iota(jnp.int32, (8, 128), 1)
    place = [p + odd * (thick - 1 - 2 * p) for p in range(thick)]

    loads = [
        pltpu.make_async_copy(hbm, ref, load_sem.at[k])
        for k, (hbm, ref) in enumerate(
            (
                (guess_hbm, guess_ref),
                (states_hbm, states_ref),
                (gain_hbm, gain_ref),
                (source_hbm, source_ref),
            )
        )
    ]
    for load in loads:
        load.start()

    def to_sibling(index, src, dst):
        return pltpu.make_async_remote_copy(
            src, dst, halo_send.at[index, 0], halo_recv.at[index, 0],
            device_id={"space": sibling}, device_id_type=MESH,
        )

    def halo_copies(index, src, view):
        off = pltpu.make_async_remote_copy(
            src, view(low), halo_send.at[index, 1], halo_recv.at[index, 1],
            device_id={"space": other}, device_id_type=MESH,
        )
        return to_sibling(index, src, view(high)), off

    def halo_start(copies):
        pl.when(has_other)(copies[1].start)
        copies[0].start()

    def to_previous(index, src, dst):
        return pltpu.make_async_remote_copy(
            src, dst, z_send.at[index], z_recv.at[index],
            device_id={"tm": t - 1}, device_id_type=MESH,
        )

    def spread_copies(index, halo_index, src, turned, wide_ref):
        straight = to_previous(index, src, wide_ref.at[heavy, own])
        across = pltpu.make_async_remote_copy(
            turned, wide_ref.at[heavy, low], z_send.at[index + 1], z_recv.at[index + 1],
            device_id={"tm": t - 1, "space": other}, device_id_type=MESH,
        )
        onward = to_sibling(halo_index, passed_on.at[index // 2], wide_ref.at[heavy, high])
        return straight, across, onward

    inv_copies = [
        halo_copies(n, inv_turned.at[n], lambda p, n=n: inv.at[n, :, p])
        for n in range(steps + 1)
    ]
    right_copies = [
        halo_copies(steps + 1 + n, right_turned.at[n], lambda p, n=n: right.at[n, :, p])
        if n == last
        else halo_copies(
            steps + 1 + n, right_turned.at[n, heavy], lambda p, n=n: right.at[n, heavy, p]
        )
        for n in range(steps)
    ]
    rest_copies = halo_copies(
        2 * steps + 1,
        right_turned.at[pl.ds(0, last), MASSIVE],
        lambda p: right.at[pl.ds(0, last), MASSIVE, p],
    )
    w_copies = spread_copies(0, 2 * steps + 2, w_src, w_turned, w_right)
    rel_copies = spread_copies(2, 2 * steps + 3, rel_src, rel_turned, rel_right)
    cor_copies = spread_copies(4, 2 * steps + 4, cor_src, cor_turned, cor_right)
    z_g = to_previous(6, g_src, g_got)
    z_rel_p0 = to_previous(7, adj.at[0], rel_p0)
    z_cor_p0 = to_previous(8, cor.at[0], cor_p0)

    rel_right[...] = jnp.zeros_like(rel_right)
    cor_right[...] = jnp.zeros_like(cor_right)

    @pl.when(jnp.logical_not(has_other))
    def _():
        inv[:, :, low] = jnp.zeros((steps + 1, FIELDS, SWEEPS, 8, 128), jnp.float32)
        right[:, :, low] = jnp.zeros((steps, FIELDS, SWEEPS, 8, 128), jnp.float32)
        w_right[:, low] = jnp.zeros((MASSIVE, SWEEPS, 8, 128), jnp.float32)

    @pl.when(t == tms - 1)
    def _():
        w_right[...] = jnp.zeros_like(w_right)
        g_got[...] = jnp.zeros_like(g_got)

    barrier = pltpu.get_barrier_semaphore()

    def greet(**device):
        pl.semaphore_signal(barrier, inc=1, device_id=device, device_id_type=MESH)

    for hop in range(1, tms):
        greet(tm=lax.rem(t + hop, tms))
    greet(space=sibling)

    @pl.when(has_other)
    def _():
        greet(space=other)
        pl.when(has_next)(lambda: greet(tm=t + 1, space=other))
        pl.when(has_prev)(lambda: greet(tm=t - 1, space=other))

    def fill_inverse(slot, n, rate):
        for i in range(FIELDS):
            base = rate * masses[i] + operator_scale * (
                (2.0 * fibre_weight + 4.0) * diffusion[i] - self_rates[i]
            )
            for p in range(thick):
                u = states_ref[n, i, place[p]].astype(jnp.float32)
                diagonal = base + state_weight * u * u - gain_weight * gain_ref[i, place[p]]
                value = 1.0 / diagonal
                inv[slot, i, first + p] = value
                inv_turned[slot, i, thick - 1 - p] = value

    loads[0].wait()
    for i in range(MASSIVE):
        for p in range(thick):
            one = guess_ref[0, 0, i, place[p]]
            value = 4.0 * one - guess_ref[0, 1, i, place[p]]
            w_src[i, p] = value
            w_turned[i, thick - 1 - p] = value
            g_src[i, p] = one
    loads[1].wait()
    loads[2].wait()
    fill_inverse(last, last, fine_rate)
    loads[3].wait()
    for i in range(FIELDS):
        for p in range(thick):
            for n in [last] if i < MASSIVE else range(steps):
                value = source_ref[n, i, place[p]]
                right[n, i, first + p] = value
                right_turned[n, i, thick - 1 - p] = value

    both = has_next.astype(jnp.int32) + has_prev.astype(jnp.int32)
    pl.semaphore_wait(barrier, tms + has_other.astype(jnp.int32) * (1 + both))

    def spread_start(copies):
        @pl.when(has_prev)
        def _():
            copies[0].start()
            pl.when(has_other)(copies[1].start)

    spread_start(w_copies)
    halo_start(inv_copies[last])
    halo_start(right_copies[last])
    pl.when(has_prev)(z_g.start)
    for n in range(last):
        fill_inverse(n, n, fine_rate)
    fill_inverse(coarse, 0, coarse_rate)

    def hand_on(copies, wide_ref, slot):
        copies[0].wait_recv()
        for i in range(MASSIVE):
            for p in range(thick):
                passed_on[slot, i, thick - 1 - p] = wide_ref[i, first + p]
        copies[2].start()

    def add_w(start):
        for i in range(MASSIVE):
            span = pl.ds(start, SWEEPS)
            right[last, i, span] = right[last, i, span] + w_right[i, span]

    def begin(rhs, factor, start, stop):
        def body(p, carry):
            for i in range(FIELDS):
                xs[0, i, p] = rhs[i, p] * factor[i, p]
            return carry

        lax.fori_loop(start, stop, body, 0, unroll=True)

    def sweep(number, rhs, factor, start, stop, result=None):
        src = xs.at[number - 1]

        def body(p, carry):
            x = [src[i, p] for i in range(FIELDS)]
            for i in range(FIELDS):
                vertical = src[i, p - 1] + src[i, p + 1]
                sides = (
                    jnp.where(row > 0, pltpu.roll(x[i], 1, 0), 0.0)
                    + jnp.where(row < 7, pltpu.roll(x[i], 7, 0), 0.0)
                    + jnp.where(col > 0, pltpu.roll(x[i], 1, 1), 0.0)
                    + jnp.where(col < 127, pltpu.roll(x[i], 127, 1), 0.0)
                )
                total = rhs[i, p] + (operator_scale * fibre_weight * diffusion[i]) * vertical
                total = total + (operator_scale * diffusion[i]) * sides
                for j in range(FIELDS):
                    if j != i:
                        total = total + (operator_scale * reaction[j][i]) * x[j]
                if result is None:
                    xs[number, i, p] = total * factor[i, p]
                else:
                    result[i, p - first] = total * factor[i, p]
            return carry

        lax.fori_loop(start, stop, body, 0, unroll=True)

    def solve(rhs, factor, result, near, far):
        begin(rhs, factor, first, end)
        sweep(1, rhs, factor, first + 1, end - 1)
        near()
        begin(rhs, factor, end, wide)
        for number in range(1, SWEEPS):
            start = end - 1 if number == 1 else first + number
            sweep(number, rhs, factor, start, wide - number)
        far()
        begin(rhs, factor, 0, first)
        for number in range(1, SWEEPS):
            sweep(number, rhs, factor, number, first + number)
        sweep(SWEEPS, rhs, factor, first, end, result)

    def wait_other(copies):
        pl.when(has_other)(copies[1].wait_recv)

    for n in range(last, -1, -1):
        if n == last:
            halo_start(inv_copies[n - 1])
            halo_start(rest_copies)

            @pl.when(has_next)
            def _():
                hand_on(w_copies, w_right, 0)

            add_w(first)
        elif n == last - 1:
            for m in range(n):
                halo_start(inv_copies[n - 1 - m])
        elif n == last - 2:
            halo_start(inv_copies[coarse])
        if n == 0:
            inv_copies[coarse][0].wait_recv()
            wait_other(inv_copies[coarse])

            @pl.when(t == tms - 1)
            def _():
                solve(rel_right, inv.at[coarse], zero_q, lambda: None, lambda: None)

        def near(n=n):
            inv_copies[n][0].wait_recv()
            if n == last - 1:
                rest_copies[0].wait_recv()
            right_copies[n][0].wait_recv()
            if n == last:
                pl.when(has_next)(w_copies[2].wait_recv)
                add_w(end)

        def far(n=n):
            wait_other(inv_copies[n])
            if n == last - 1:
                wait_other(rest_copies)
            wait_other(right_copies[n])
            if n == last:
                pl.when(jnp.logical_and(has_next, has_other))(w_copies[1].wait_recv)
                add_w(0)

        solve(right.at[n], inv.at[n], adj.at[n], near, far)
        if n == last:
            pl.when(has_next)(z_g.wait_recv)
        if n > 0:
            for i in range(MASSIVE):
                for p in range(thick):
                    before = g_got[i, p] if n == last else adj[n + 1, i, p]
                    value = source_ref[n - 1, i, place[p]] + (4.0 * adj[n, i, p] - before)
                    right[n - 1, i, first + p] = value
                    right_turned[n - 1, i, thick - 1 - p] = value
            halo_start(right_copies[n - 1])
        else:
            for i in range(MASSIVE):
                for p in range(thick):
                    value = adj[0, i, p] - 0.25 * adj[1, i, p]
                    rel_src[i, p] = value
                    rel_turned[i, thick - 1 - p] = value
            spread_start(rel_copies)

            @pl.when(jnp.logical_and(has_prev, has_next))
            def _():
                z_rel_p0.start()

    def send_corrected():
        for i in range(MASSIVE):
            for p in range(thick):
                value = cor[0, i, p] - 0.25 * cor[1, i, p]
                cor_src[i, p] = value
                cor_turned[i, thick - 1 - p] = value
        spread_start(cor_copies)

    @pl.when(t == tms - 1)
    def _():
        for i in range(FIELDS):
            zero_p1 = 0.5 * (zero_q[i] + 0.0)
            cor[0, i] = zero_q[i] + (adj[0, i] - zero_q[i])
            cor[1, i] = zero_p1 + (adj[1, i] - zero_p1)
        send_corrected()

        @pl.when(has_prev)
        def _():
            z_rel_p0.start()
            z_cor_p0.start()

    for n in range(last, -1, -1):
        for i in range(FIELDS):
            for p in range(thick):
                term = adj[n, i, p] * states_ref[n, i, place[p]].astype(jnp.float32)
                spot = i * thick + p
                part[spot] = term if n == last else part[spot] + term

    chunk = FIELDS * thick // tms
    grad_one, grad_two, grad_in = [], [], []
    for hop in range(1, tms):
        target = lax.rem(t + hop, tms)
        origin = lax.rem(t + tms - hop, tms)
        grad_one.append(
            pltpu.make_async_remote_copy(
                part.at[pl.ds(target * chunk, chunk)], part_got.at[hop - 1],
                grad_send.at[0, hop - 1], grad_recv.at[0, hop - 1],
                device_id={"tm": target}, device_id_type=MESH,
            )
        )
        mine = whole.at[pl.ds(t * chunk, chunk)]
        grad_two.append(
            pltpu.make_async_remote_copy(
                mine, mine, grad_send.at[1, hop - 1], grad_recv.at[1, hop - 1],
                device_id={"tm": target}, device_id_type=MESH,
            )
        )
        theirs = whole.at[pl.ds(origin * chunk, chunk)]
        grad_in.append(
            pltpu.make_async_remote_copy(
                theirs, theirs, grad_send.at[1, hop - 1], grad_recv.at[1, hop - 1],
                device_id={"tm": target}, device_id_type=MESH,
            )
        )
    for copy in grad_one:
        copy.start()

    @pl.when(has_next)
    def _():
        hand_on(rel_copies, rel_right, 1)

        @pl.when(t == tms - 2)
        def _():
            hand_on(cor_copies, cor_right, 2)

        def far():
            pl.when(has_other)(rel_copies[1].wait_recv)

        solve(rel_right, inv.at[coarse], rel_q, rel_copies[2].wait_recv, far)
        z_rel_p0.wait_recv()
        for i in range(FIELDS):
            offs[0, i] = adj[0, i] - rel_q[i]
            offs[1, i] = adj[1, i] - 0.5 * (rel_q[i] + rel_p0[i])

    def share_gradient():
        for copy in grad_one:
            copy.wait_recv()
        total = part[pl.ds(t * chunk, chunk)]
        for hop in range(1, tms):
            total = total + part_got[hop - 1]
        whole[pl.ds(t * chunk, chunk)] = time_step * total
        for copy in grad_two:
            copy.start()

    pl.when(jnp.logical_or(t < tms - 2, t == tms - 1))(share_gradient)

    @pl.when(has_next)
    def _():
        @pl.when(t < tms - 2)
        def _():
            hand_on(cor_copies, cor_right, 2)

        def far():
            pl.when(has_other)(cor_copies[1].wait_recv)

        solve(cor_right, inv.at[coarse], cor_q, cor_copies[2].wait_recv, far)
        z_cor_p0.wait_recv()
        for i in range(FIELDS):
            cor[0, i] = cor_q[i] + offs[0, i]
            cor[1, i] = 0.5 * (cor_q[i] + cor_p0[i]) + offs[1, i]
        send_corrected()
        pl.when(has_prev)(z_cor_p0.start)

    pl.when(t == tms - 2)(share_gradient)

    for pair in range(2):
        for i in range(FIELDS):
            for p in range(thick):
                corrected_ref[0, pair, i, place[p]] = cor[pair, i, p]
    for copy in grad_in:
        copy.wait_recv()
    for i in range(FIELDS):
        for p in range(thick):
            gradient_ref[i, place[p]] = whole[i * thick + p]

    halos = inv_copies + right_copies + [rest_copies]
    for copies in halos:
        copies[0].wait_send()

    @pl.when(has_other)
    def _():
        for copies in halos:
            copies[1].wait_send()

    @pl.when(has_next)
    def _():
        for copies in (w_copies, rel_copies, cor_copies):
            copies[2].wait_send()

    @pl.when(has_prev)
    def _():
        for copies in (w_copies, rel_copies, cor_copies):
            copies[0].wait_send()
            pl.when(has_other)(copies[1].wait_send)
        for copy in (z_g, z_rel_p0, z_cor_p0):
            copy.wait_send()

    for copy in grad_one + grad_two:
        copy.wait_send()


def on_device(tms, spaces, forward_states, adjoint_source, source_gain, guess_pairs):
    steps, _, thick = forward_states.shape[:3]
    wide = thick + 2 * SWEEPS
    vmem = lambda *shape: pltpu.VMEM(shape + (8, 128), jnp.float32)
    chunk = FIELDS * thick // tms
    in_vmem = pl.BlockSpec(memory_space=pltpu.VMEM)
    heavy = vmem(MASSIVE, thick)
    every = vmem(FIELDS, thick)
    return pl.pallas_call(
        functools.partial(kernel, steps, thick, tms, spaces),
        out_shape=(
            jax.ShapeDtypeStruct(guess_pairs.shape, jnp.float32),
            jax.ShapeDtypeStruct(source_gain.shape, jnp.float32),
        ),
        in_specs=[pl.BlockSpec(memory_space=pl.ANY)] * 4,
        out_specs=(in_vmem, in_vmem),
        scratch_shapes=[
            pltpu.VMEM(forward_states.shape, forward_states.dtype),
            pltpu.VMEM(adjoint_source.shape, jnp.float32),
            pltpu.VMEM(source_gain.shape, jnp.float32),
            pltpu.VMEM(guess_pairs.shape, jnp.float32),
            vmem(steps + 1, FIELDS, wide),
            vmem(steps + 1, FIELDS, thick),
            vmem(steps, FIELDS, wide),
            vmem(steps, FIELDS, thick),
            vmem(MASSIVE, wide),
            vmem(FIELDS, wide),
            vmem(FIELDS, wide),
            vmem(SWEEPS, FIELDS, wide),
            vmem(steps, FIELDS, thick),
            every,
            every,
            every,
            vmem(2, FIELDS, thick),
            vmem(2, FIELDS, thick),
            heavy,
            heavy,
            heavy,
            heavy,
            heavy,
            heavy,
            every,
            heavy,
            heavy,
            every,
            vmem(3, MASSIVE, thick),
            vmem(FIELDS * thick),
            vmem(tms - 1, chunk),
            vmem(FIELDS * thick),
            pltpu.SemaphoreType.DMA((4,)),
            pltpu.SemaphoreType.DMA((2 * steps + 5, 2)),
            pltpu.SemaphoreType.DMA((2 * steps + 5, 2)),
            pltpu.SemaphoreType.DMA((9,)),
            pltpu.SemaphoreType.DMA((9,)),
            pltpu.SemaphoreType.DMA((2, tms - 1)),
            pltpu.SemaphoreType.DMA((2, tms - 1)),
        ],
        compiler_params=pltpu.CompilerParams(
            collective_id=0, has_side_effects=True, vmem_limit_bytes=32 * 1024 * 1024
        ),
        name="adjoint_cycle",
    )(forward_states, adjoint_source, source_gain, guess_pairs)


def solution(mesh):
    placed = (
        P("tm", None, "space", None, None),
        P("tm", None, "space", None, None),
        P(None, "space", None, None),
        P("tm", None, None, "space", None, None),
    )
    return jax.shard_map(
        functools.partial(on_device, mesh.shape["tm"], mesh.shape["space"]),
        mesh=mesh,
        in_specs=placed,
        out_specs=(P("tm", None, None, "space", None, None), P(None, "space", None, None)),
        check_vma=False,
    )
```

```python
import functools

import jax
import jax.numpy as jnp
from jax import lax
from jax.experimental import pallas as pl
from jax.experimental.pallas import tpu as pltpu
from jax.sharding import PartitionSpec as P

SWEEPS = 4
FIELDS = 4
MASSIVE = 3

diffusion = (2.4, 1.2, 0.6, 4.0)
fibre_weight = 128.0
reaction = (
    (-14.4, 7.2, -4.8, 2.4),
    (4.8, -19.2, 7.2, -4.8),
    (-7.2, 2.4, -12.0, 7.2),
    (4.8, -7.2, 2.4, -38.4),
)
self_rates = (-14.4, -19.2, -12.0, -38.4)
masses = (1.0, 1.0, 1.0, 0.0)
fine_rate = 3.0
coarse_rate = 0.75
time_step = 0.5
operator_scale = 0.0078125
state_weight = 0.1
gain_weight = 0.25

MESH = pl.DeviceIdType.MESH


def kernel(
    steps, thick, tms, spaces,
    states_hbm, source_hbm, gain_hbm, guess_hbm,
    corrected_ref, gradient_ref,
    states_ref, source_ref, gain_ref, guess_ref,
    inv, inv_turned, right, right_turned, w_right, rel_right, cor_right, xs,
    adj, zero_q, rel_q, cor_q, offs, cor,
    w_src, w_turned, g_src, g_got, rel_src, rel_turned, rel_p0, cor_src, cor_turned, cor_p0,
    passed_on, part, part_got, whole,
    load_sem, halo_send, halo_recv, z_send, z_recv, grad_send, grad_recv,
):
    t = lax.axis_index("tm")
    s = lax.axis_index("space")
    odd = lax.rem(s, 2)
    sibling = s + 1 - 2 * odd
    other = s - 1 + 2 * odd
    has_other = jnp.logical_and(other >= 0, other < spaces)
    has_next, has_prev = t < tms - 1, t > 0
    wide = thick + 2 * SWEEPS
    first, end = SWEEPS, SWEEPS + thick
    own = pl.ds(SWEEPS, thick)
    low = pl.ds(0, SWEEPS)
    high = pl.ds(SWEEPS + thick, SWEEPS)
    heavy = pl.ds(0, MASSIVE)
    coarse = steps
    last = steps - 1
    row = lax.broadcasted_iota(jnp.int32, (8, 128), 0)
    col = lax.broadcasted_iota(jnp.int32, (8, 128), 1)
    place = [p + odd * (thick - 1 - 2 * p) for p in range(thick)]

    loads = [
        pltpu.make_async_copy(hbm, ref, load_sem.at[k])
        for k, (hbm, ref) in enumerate(
            (
                (guess_hbm, guess_ref),
                (states_hbm, states_ref),
                (gain_hbm, gain_ref),
                (source_hbm, source_ref),
            )
        )
    ]
    for load in loads:
        load.start()

    def to_sibling(index, src, dst):
        return pltpu.make_async_remote_copy(
            src, dst, halo_send.at[index, 0], halo_recv.at[index, 0],
            device_id={"space": sibling}, device_id_type=MESH,
        )

    def halo_copies(index, src, view):
        off = pltpu.make_async_remote_copy(
            src, view(low), halo_send.at[index, 1], halo_recv.at[index, 1],
            device_id={"space": other}, device_id_type=MESH,
        )
        return to_sibling(index, src, view(high)), off

    def halo_start(copies):
        pl.when(has_other)(copies[1].start)
        copies[0].start()

    def to_previous(index, src, dst):
        return pltpu.make_async_remote_copy(
            src, dst, z_send.at[index], z_recv.at[index],
            device_id={"tm": t - 1}, device_id_type=MESH,
        )

    def spread_copies(index, halo_index, src, turned, wide_ref):
        straight = to_previous(index, src, wide_ref.at[heavy, own])
        across = pltpu.make_async_remote_copy(
            turned, wide_ref.at[heavy, low], z_send.at[index + 1], z_recv.at[index + 1],
            device_id={"tm": t - 1, "space": other}, device_id_type=MESH,
        )
        onward = to_sibling(halo_index, passed_on.at[index // 2], wide_ref.at[heavy, high])
        return straight, across, onward

    inv_copies = [
        halo_copies(n, inv_turned.at[n], lambda p, n=n: inv.at[n, :, p])
        for n in range(steps)
    ]
    right_copies = [
        halo_copies(steps + 1 + n, right_turned.at[n], lambda p, n=n: right.at[n, :, p])
        if n == last
        else halo_copies(
            steps + 1 + n, right_turned.at[n, heavy], lambda p, n=n: right.at[n, heavy, p]
        )
        for n in range(steps)
    ]
    rest_copies = halo_copies(
        2 * steps + 1,
        right_turned.at[pl.ds(0, last), MASSIVE],
        lambda p: right.at[pl.ds(0, last), MASSIVE, p],
    )
    w_copies = spread_copies(0, 2 * steps + 2, w_src, w_turned, w_right)
    rel_copies = spread_copies(2, 2 * steps + 3, rel_src, rel_turned, rel_right)
    cor_copies = spread_copies(4, 2 * steps + 4, cor_src, cor_turned, cor_right)
    z_g = to_previous(6, g_src, g_got)
    z_rel_p0 = to_previous(7, adj.at[0], rel_p0)
    z_cor_p0 = to_previous(8, cor.at[0], cor_p0)

    rel_right[...] = jnp.zeros_like(rel_right)
    cor_right[...] = jnp.zeros_like(cor_right)

    @pl.when(jnp.logical_not(has_other))
    def _():
        inv[:, :, low] = jnp.zeros((steps + 1, FIELDS, SWEEPS, 8, 128), jnp.float32)
        right[:, :, low] = jnp.zeros((steps, FIELDS, SWEEPS, 8, 128), jnp.float32)
        w_right[:, low] = jnp.zeros((MASSIVE, SWEEPS, 8, 128), jnp.float32)

    @pl.when(t == tms - 1)
    def _():
        w_right[...] = jnp.zeros_like(w_right)
        g_got[...] = jnp.zeros_like(g_got)

    barrier = pltpu.get_barrier_semaphore()

    def greet(**device):
        pl.semaphore_signal(barrier, inc=1, device_id=device, device_id_type=MESH)

    for hop in range(1, tms):
        greet(tm=lax.rem(t + hop, tms))
    greet(space=sibling)

    @pl.when(has_other)
    def _():
        greet(space=other)
        pl.when(has_next)(lambda: greet(tm=t + 1, space=other))
        pl.when(has_prev)(lambda: greet(tm=t - 1, space=other))

    def fill_inverse(slot, n, rate):
        for i in range(FIELDS):
            base = rate * masses[i] + operator_scale * (
                (2.0 * fibre_weight + 4.0) * diffusion[i] - self_rates[i]
            )
            for p in range(thick):
                u = states_ref[n, i, place[p]].astype(jnp.float32)
                diagonal = base + state_weight * u * u - gain_weight * gain_ref[i, place[p]]
                value = 1.0 / diagonal
                inv[slot, i, first + p] = value
                if slot < steps:
                    inv_turned[slot, i, thick - 1 - p] = diagonal if slot == 0 else value

    loads[0].wait()
    for i in range(MASSIVE):
        for p in range(thick):
            one = guess_ref[0, 0, i, place[p]]
            value = 4.0 * one - guess_ref[0, 1, i, place[p]]
            w_src[i, p] = value
            w_turned[i, thick - 1 - p] = value
            g_src[i, p] = one
    loads[1].wait()
    loads[2].wait()
    fill_inverse(last, last, fine_rate)
    loads[3].wait()
    for i in range(FIELDS):
        for p in range(thick):
            for n in [last] if i < MASSIVE else range(steps):
                value = source_ref[n, i, place[p]]
                right[n, i, first + p] = value
                right_turned[n, i, thick - 1 - p] = value

    both = has_next.astype(jnp.int32) + has_prev.astype(jnp.int32)
    pl.semaphore_wait(barrier, tms + has_other.astype(jnp.int32) * (1 + both))

    def spread_start(copies):
        @pl.when(has_prev)
        def _():
            copies[0].start()
            pl.when(has_other)(copies[1].start)

    spread_start(w_copies)
    halo_start(inv_copies[last])
    halo_start(right_copies[last])
    pl.when(has_prev)(z_g.start)
    for n in range(last):
        fill_inverse(n, n, fine_rate)
    fill_inverse(coarse, 0, coarse_rate)

    def invert_first(start):
        for i in range(FIELDS):
            for p in range(start, start + SWEEPS):
                diagonal = inv[0, i, p]
                inv[coarse, i, p] = 1.0 / (diagonal - (fine_rate - coarse_rate) * masses[i])
                inv[0, i, p] = 1.0 / diagonal

    def hand_on(copies, wide_ref, slot):
        copies[0].wait_recv()
        for i in range(MASSIVE):
            for p in range(thick):
                passed_on[slot, i, thick - 1 - p] = wide_ref[i, first + p]
        copies[2].start()

    def add_w(start):
        for i in range(MASSIVE):
            span = pl.ds(start, SWEEPS)
            right[last, i, span] = right[last, i, span] + w_right[i, span]

    def begin(rhs, factor, start, stop):
        def body(p, carry):
            for i in range(FIELDS):
                xs[0, i, p] = rhs[i, p] * factor[i, p]
            return carry

        lax.fori_loop(start, stop, body, 0, unroll=True)

    def sweep(number, rhs, factor, start, stop, result=None):
        src = xs.at[number - 1]

        def body(p, carry):
            x = [src[i, p] for i in range(FIELDS)]
            for i in range(FIELDS):
                vertical = src[i, p - 1] + src[i, p + 1]
                total = rhs[i, p] + (operator_scale * fibre_weight * diffusion[i]) * vertical
                mixed = None
                for j in range(FIELDS):
                    if j != i:
                        term = (operator_scale * reaction[j][i]) * x[j]
                        mixed = term if mixed is None else mixed + term
                total = total + mixed
                along = jnp.where(row > 0, pltpu.roll(x[i], 1, 0), 0.0) + jnp.where(
                    row < 7, pltpu.roll(x[i], 7, 0), 0.0
                )
                across = jnp.where(col > 0, pltpu.roll(x[i], 1, 1), 0.0) + jnp.where(
                    col < 127, pltpu.roll(x[i], 127, 1), 0.0
                )
                total = total + (operator_scale * diffusion[i]) * (along + across)
                if result is None:
                    xs[number, i, p] = total * factor[i, p]
                else:
                    result[i, p - first] = total * factor[i, p]
            return carry

        lax.fori_loop(start, stop, body, 0, unroll=True)

    def solve(rhs, factor, result, near, far):
        begin(rhs, factor, first, end)
        sweep(1, rhs, factor, first + 1, end - 1)
        near()
        begin(rhs, factor, end, wide)
        for number in range(1, SWEEPS):
            start = end - 1 if number == 1 else first + number
            sweep(number, rhs, factor, start, wide - number)
        far()
        begin(rhs, factor, 0, first)
        for number in range(1, SWEEPS):
            sweep(number, rhs, factor, number, first + number)
        sweep(SWEEPS, rhs, factor, first, end, result)

    def wait_other(copies):
        pl.when(has_other)(copies[1].wait_recv)

    for n in range(last, -1, -1):
        if n == last:
            halo_start(inv_copies[n - 1])
            halo_start(rest_copies)

            @pl.when(has_next)
            def _():
                hand_on(w_copies, w_right, 0)

            add_w(first)
        elif n == last - 1:
            for m in range(n):
                halo_start(inv_copies[n - 1 - m])
        if n == 0:
            inv_copies[0][0].wait_recv()
            invert_first(end)

            @pl.when(has_other)
            def _():
                inv_copies[0][1].wait_recv()
                invert_first(0)

            @pl.when(t == tms - 1)
            def _():
                solve(rel_right, inv.at[coarse], zero_q, lambda: None, lambda: None)

        def near(n=n):
            if n > 0:
                inv_copies[n][0].wait_recv()
            if n == last - 1:
                rest_copies[0].wait_recv()
            right_copies[n][0].wait_recv()
            if n == last:
                pl.when(has_next)(w_copies[2].wait_recv)
                add_w(end)

        def far(n=n):
            if n > 0:
                wait_other(inv_copies[n])
            if n == last - 1:
                wait_other(rest_copies)
            wait_other(right_copies[n])
            if n == last:
                pl.when(jnp.logical_and(has_next, has_other))(w_copies[1].wait_recv)
                add_w(0)

        solve(right.at[n], inv.at[n], adj.at[n], near, far)
        if n == last:
            pl.when(has_next)(z_g.wait_recv)
        if n > 0:
            for i in range(MASSIVE):
                for p in range(thick):
                    before = g_got[i, p] if n == last else adj[n + 1, i, p]
                    value = source_ref[n - 1, i, place[p]] + (4.0 * adj[n, i, p] - before)
                    right[n - 1, i, first + p] = value
                    right_turned[n - 1, i, thick - 1 - p] = value
            halo_start(right_copies[n - 1])
        else:
            for i in range(MASSIVE):
                for p in range(thick):
                    value = adj[0, i, p] - 0.25 * adj[1, i, p]
                    rel_src[i, p] = value
                    rel_turned[i, thick - 1 - p] = value
            spread_start(rel_copies)

            @pl.when(jnp.logical_and(has_prev, has_next))
            def _():
                z_rel_p0.start()

    def send_corrected():
        for i in range(MASSIVE):
            for p in range(thick):
                value = cor[0, i, p] - 0.25 * cor[1, i, p]
                cor_src[i, p] = value
                cor_turned[i, thick - 1 - p] = value
        spread_start(cor_copies)

    @pl.when(t == tms - 1)
    def _():
        for i in range(FIELDS):
            zero_p1 = 0.5 * (zero_q[i] + 0.0)
            cor[0, i] = zero_q[i] + (adj[0, i] - zero_q[i])
            cor[1, i] = zero_p1 + (adj[1, i] - zero_p1)
        send_corrected()

        @pl.when(has_prev)
        def _():
            z_rel_p0.start()
            z_cor_p0.start()

    for n in range(last, -1, -1):
        for i in range(FIELDS):
            for p in range(thick):
                term = adj[n, i, p] * states_ref[n, i, place[p]].astype(jnp.float32)
                spot = i * thick + p
                part[spot] = term if n == last else part[spot] + term

    chunk = FIELDS * thick // tms
    grad_one, grad_two, grad_in = [], [], []
    for hop in range(1, tms):
        target = lax.rem(t + hop, tms)
        origin = lax.rem(t + tms - hop, tms)
        grad_one.append(
            pltpu.make_async_remote_copy(
                part.at[pl.ds(target * chunk, chunk)], part_got.at[hop - 1],
                grad_send.at[0, hop - 1], grad_recv.at[0, hop - 1],
                device_id={"tm": target}, device_id_type=MESH,
            )
        )
        mine = whole.at[pl.ds(t * chunk, chunk)]
        grad_two.append(
            pltpu.make_async_remote_copy(
                mine, mine, grad_send.at[1, hop - 1], grad_recv.at[1, hop - 1],
                device_id={"tm": target}, device_id_type=MESH,
            )
        )
        theirs = whole.at[pl.ds(origin * chunk, chunk)]
        grad_in.append(
            pltpu.make_async_remote_copy(
                theirs, theirs, grad_send.at[1, hop - 1], grad_recv.at[1, hop - 1],
                device_id={"tm": target}, device_id_type=MESH,
            )
        )
    for copy in grad_one:
        copy.start()

    @pl.when(has_next)
    def _():
        hand_on(rel_copies, rel_right, 1)

        @pl.when(t == tms - 2)
        def _():
            hand_on(cor_copies, cor_right, 2)

        def far():
            pl.when(has_other)(rel_copies[1].wait_recv)

        solve(rel_right, inv.at[coarse], rel_q, rel_copies[2].wait_recv, far)
        z_rel_p0.wait_recv()
        for i in range(FIELDS):
            offs[0, i] = adj[0, i] - rel_q[i]
            offs[1, i] = adj[1, i] - 0.5 * (rel_q[i] + rel_p0[i])

    def share_gradient():
        for copy in grad_one:
            copy.wait_recv()
        total = part[pl.ds(t * chunk, chunk)]
        for hop in range(1, tms):
            total = total + part_got[hop - 1]
        whole[pl.ds(t * chunk, chunk)] = time_step * total
        for copy in grad_two:
            copy.start()

    pl.when(jnp.logical_or(t < tms - 2, t == tms - 1))(share_gradient)

    @pl.when(has_next)
    def _():
        @pl.when(t < tms - 2)
        def _():
            hand_on(cor_copies, cor_right, 2)

        def far():
            pl.when(has_other)(cor_copies[1].wait_recv)

        solve(cor_right, inv.at[coarse], cor_q, cor_copies[2].wait_recv, far)
        z_cor_p0.wait_recv()
        for i in range(FIELDS):
            cor[0, i] = cor_q[i] + offs[0, i]
            cor[1, i] = 0.5 * (cor_q[i] + cor_p0[i]) + offs[1, i]
        send_corrected()
        pl.when(has_prev)(z_cor_p0.start)

    pl.when(t == tms - 2)(share_gradient)

    for pair in range(2):
        for i in range(FIELDS):
            for p in range(thick):
                corrected_ref[0, pair, i, place[p]] = cor[pair, i, p]
    for copy in grad_in:
        copy.wait_recv()
    for i in range(FIELDS):
        for p in range(thick):
            gradient_ref[i, place[p]] = whole[i * thick + p]

    halos = inv_copies + right_copies + [rest_copies]
    for copies in halos:
        copies[0].wait_send()

    @pl.when(has_other)
    def _():
        for copies in halos:
            copies[1].wait_send()

    @pl.when(has_next)
    def _():
        for copies in (w_copies, rel_copies, cor_copies):
            copies[2].wait_send()

    @pl.when(has_prev)
    def _():
        for copies in (w_copies, rel_copies, cor_copies):
            copies[0].wait_send()
            pl.when(has_other)(copies[1].wait_send)
        for copy in (z_g, z_rel_p0, z_cor_p0):
            copy.wait_send()

    for copy in grad_one + grad_two:
        copy.wait_send()


def on_device(tms, spaces, forward_states, adjoint_source, source_gain, guess_pairs):
    steps, _, thick = forward_states.shape[:3]
    wide = thick + 2 * SWEEPS
    vmem = lambda *shape: pltpu.VMEM(shape + (8, 128), jnp.float32)
    chunk = FIELDS * thick // tms
    in_vmem = pl.BlockSpec(memory_space=pltpu.VMEM)
    heavy = vmem(MASSIVE, thick)
    every = vmem(FIELDS, thick)
    return pl.pallas_call(
        functools.partial(kernel, steps, thick, tms, spaces),
        out_shape=(
            jax.ShapeDtypeStruct(guess_pairs.shape, jnp.float32),
            jax.ShapeDtypeStruct(source_gain.shape, jnp.float32),
        ),
        in_specs=[pl.BlockSpec(memory_space=pltpu.HBM)] * 4,
        out_specs=(in_vmem, in_vmem),
        scratch_shapes=[
            pltpu.VMEM(forward_states.shape, forward_states.dtype),
            pltpu.VMEM(adjoint_source.shape, jnp.float32),
            pltpu.VMEM(source_gain.shape, jnp.float32),
            pltpu.VMEM(guess_pairs.shape, jnp.float32),
            vmem(steps + 1, FIELDS, wide),
            vmem(steps, FIELDS, thick),
            vmem(steps, FIELDS, wide),
            vmem(steps, FIELDS, thick),
            vmem(MASSIVE, wide),
            vmem(FIELDS, wide),
            vmem(FIELDS, wide),
            vmem(SWEEPS, FIELDS, wide),
            vmem(steps, FIELDS, thick),
            every,
            every,
            every,
            vmem(2, FIELDS, thick),
            vmem(2, FIELDS, thick),
            heavy,
            heavy,
            heavy,
            heavy,
            heavy,
            heavy,
            every,
            heavy,
            heavy,
            every,
            vmem(3, MASSIVE, thick),
            vmem(FIELDS * thick),
            vmem(tms - 1, chunk),
            vmem(FIELDS * thick),
            pltpu.SemaphoreType.DMA((4,)),
            pltpu.SemaphoreType.DMA((2 * steps + 5, 2)),
            pltpu.SemaphoreType.DMA((2 * steps + 5, 2)),
            pltpu.SemaphoreType.DMA((9,)),
            pltpu.SemaphoreType.DMA((9,)),
            pltpu.SemaphoreType.DMA((2, tms - 1)),
            pltpu.SemaphoreType.DMA((2, tms - 1)),
        ],
        compiler_params=pltpu.CompilerParams(
            collective_id=0, has_side_effects=True, vmem_limit_bytes=64 * 1024 * 1024
        ),
        name="adjoint_cycle",
    )(forward_states, adjoint_source, source_gain, guess_pairs)


def solution(mesh):
    placed = (
        P("tm", None, "space", None, None),
        P("tm", None, "space", None, None),
        P(None, "space", None, None),
        P("tm", None, None, "space", None, None),
    )
    return jax.shard_map(
        functools.partial(on_device, mesh.shape["tm"], mesh.shape["space"]),
        mesh=mesh,
        in_specs=placed,
        out_specs=(P("tm", None, None, "space", None, None), P(None, "space", None, None)),
        check_vma=False,
    )
```

```python
import functools

import jax
import jax.numpy as jnp
from jax import lax
from jax.experimental import pallas as pl
from jax.experimental.pallas import tpu as pltpu
from jax.sharding import PartitionSpec as P

SWEEPS = 4
FIELDS = 4
MASSIVE = 3

diffusion = (2.4, 1.2, 0.6, 4.0)
fibre_weight = 128.0
reaction = (
    (-14.4, 7.2, -4.8, 2.4),
    (4.8, -19.2, 7.2, -4.8),
    (-7.2, 2.4, -12.0, 7.2),
    (4.8, -7.2, 2.4, -38.4),
)
self_rates = (-14.4, -19.2, -12.0, -38.4)
masses = (1.0, 1.0, 1.0, 0.0)
fine_rate = 3.0
coarse_rate = 0.75
time_step = 0.5
operator_scale = 0.0078125
state_weight = 0.1
gain_weight = 0.25

MESH = pl.DeviceIdType.MESH


def kernel(
    steps, thick, tms, spaces,
    states_hbm, source_hbm, gain_hbm, guess_hbm,
    corrected_ref, gradient_ref,
    states_ref, source_ref, gain_ref, guess_ref,
    inv, inv_turned, right, right_turned, w_right, rel_right, cor_right, xs,
    adj, zero_q, rel_q, cor_q, offs, cor,
    w_src, w_turned, g_src, g_got, rel_src, rel_turned, cor_src, cor_turned, change, change_got,
    passed_on, part, part_got, whole,
    load_sem, halo_send, halo_recv, z_send, z_recv, grad_send, grad_recv,
):
    t = lax.axis_index("tm")
    s = lax.axis_index("space")
    odd = lax.rem(s, 2)
    sibling = s + 1 - 2 * odd
    other = s - 1 + 2 * odd
    has_other = jnp.logical_and(other >= 0, other < spaces)
    has_next, has_prev = t < tms - 1, t > 0
    wide = thick + 2 * SWEEPS
    first, end = SWEEPS, SWEEPS + thick
    own = pl.ds(SWEEPS, thick)
    low = pl.ds(0, SWEEPS)
    high = pl.ds(SWEEPS + thick, SWEEPS)
    heavy = pl.ds(0, MASSIVE)
    coarse = steps
    last = steps - 1
    row = lax.broadcasted_iota(jnp.int32, (8, 128), 0)
    col = lax.broadcasted_iota(jnp.int32, (8, 128), 1)
    place = [p + odd * (thick - 1 - 2 * p) for p in range(thick)]

    loads = [
        pltpu.make_async_copy(hbm, ref, load_sem.at[k])
        for k, (hbm, ref) in enumerate(
            (
                (guess_hbm, guess_ref),
                (states_hbm, states_ref),
                (gain_hbm, gain_ref),
                (source_hbm, source_ref),
            )
        )
    ]
    for load in loads:
        load.start()

    def to_sibling(index, src, dst):
        return pltpu.make_async_remote_copy(
            src, dst, halo_send.at[index, 0], halo_recv.at[index, 0],
            device_id={"space": sibling}, device_id_type=MESH,
        )

    def halo_copies(index, src, view):
        off = pltpu.make_async_remote_copy(
            src, view(low), halo_send.at[index, 1], halo_recv.at[index, 1],
            device_id={"space": other}, device_id_type=MESH,
        )
        return to_sibling(index, src, view(high)), off

    def halo_start(copies):
        pl.when(has_other)(copies[1].start)
        copies[0].start()

    def to_previous(index, src, dst):
        return pltpu.make_async_remote_copy(
            src, dst, z_send.at[index], z_recv.at[index],
            device_id={"tm": t - 1}, device_id_type=MESH,
        )

    def spread_copies(index, halo_index, src, turned, wide_ref):
        straight = to_previous(index, src, wide_ref.at[heavy, own])
        across = pltpu.make_async_remote_copy(
            turned, wide_ref.at[heavy, low], z_send.at[index + 1], z_recv.at[index + 1],
            device_id={"tm": t - 1, "space": other}, device_id_type=MESH,
        )
        onward = to_sibling(halo_index, passed_on.at[index // 2], wide_ref.at[heavy, high])
        return straight, across, onward

    inv_copies = [
        halo_copies(n, inv_turned.at[n], lambda p, n=n: inv.at[n, :, p])
        for n in range(steps)
    ]
    right_copies = [
        halo_copies(steps + 1 + n, right_turned.at[n], lambda p, n=n: right.at[n, :, p])
        if n == last
        else halo_copies(
            steps + 1 + n, right_turned.at[n, heavy], lambda p, n=n: right.at[n, heavy, p]
        )
        for n in range(steps)
    ]
    rest_copies = halo_copies(
        2 * steps + 1,
        right_turned.at[pl.ds(0, last), MASSIVE],
        lambda p: right.at[pl.ds(0, last), MASSIVE, p],
    )
    w_copies = spread_copies(0, 2 * steps + 2, w_src, w_turned, w_right)
    rel_copies = spread_copies(2, 2 * steps + 3, rel_src, rel_turned, rel_right)
    cor_copies = spread_copies(4, 2 * steps + 4, cor_src, cor_turned, cor_right)
    z_g = to_previous(6, g_src, g_got)
    z_change = to_previous(7, change, change_got)

    rel_right[...] = jnp.zeros_like(rel_right)
    cor_right[...] = jnp.zeros_like(cor_right)

    @pl.when(jnp.logical_not(has_other))
    def _():
        inv[:, :, low] = jnp.zeros((steps + 1, FIELDS, SWEEPS, 8, 128), jnp.float32)
        right[:, :, low] = jnp.zeros((steps, FIELDS, SWEEPS, 8, 128), jnp.float32)
        w_right[:, low] = jnp.zeros((MASSIVE, SWEEPS, 8, 128), jnp.float32)

    @pl.when(t == tms - 1)
    def _():
        w_right[...] = jnp.zeros_like(w_right)
        g_got[...] = jnp.zeros_like(g_got)

    barrier = pltpu.get_barrier_semaphore()

    def greet(**device):
        pl.semaphore_signal(barrier, inc=1, device_id=device, device_id_type=MESH)

    for hop in range(1, tms):
        greet(tm=lax.rem(t + hop, tms))
    greet(space=sibling)

    @pl.when(has_other)
    def _():
        greet(space=other)
        pl.when(has_next)(lambda: greet(tm=t + 1, space=other))
        pl.when(has_prev)(lambda: greet(tm=t - 1, space=other))

    def fill_inverse(slot, n, rate):
        for i in range(FIELDS):
            base = rate * masses[i] + operator_scale * (
                (2.0 * fibre_weight + 4.0) * diffusion[i] - self_rates[i]
            )
            for p in range(thick):
                u = states_ref[n, i, place[p]].astype(jnp.float32)
                diagonal = base + state_weight * u * u - gain_weight * gain_ref[i, place[p]]
                value = 1.0 / diagonal
                inv[slot, i, first + p] = value
                if slot < steps:
                    inv_turned[slot, i, thick - 1 - p] = diagonal if slot == 0 else value

    loads[0].wait()
    for i in range(MASSIVE):
        for p in range(thick):
            one = guess_ref[0, 0, i, place[p]]
            value = 4.0 * one - guess_ref[0, 1, i, place[p]]
            w_src[i, p] = value
            w_turned[i, thick - 1 - p] = value
            g_src[i, p] = one
    loads[1].wait()
    loads[2].wait()
    fill_inverse(last, last, fine_rate)
    loads[3].wait()
    for i in range(FIELDS):
        for p in range(thick):
            for n in [last] if i < MASSIVE else range(steps):
                value = source_ref[n, i, place[p]]
                right[n, i, first + p] = value
                right_turned[n, i, thick - 1 - p] = value

    both = has_next.astype(jnp.int32) + has_prev.astype(jnp.int32)
    pl.semaphore_wait(barrier, tms + has_other.astype(jnp.int32) * (1 + both))

    def spread_start(copies):
        @pl.when(has_prev)
        def _():
            copies[0].start()
            pl.when(has_other)(copies[1].start)

    spread_start(w_copies)
    halo_start(inv_copies[last])
    halo_start(right_copies[last])
    pl.when(has_prev)(z_g.start)
    for n in range(last):
        fill_inverse(n, n, fine_rate)
    fill_inverse(coarse, 0, coarse_rate)

    def invert_first(start):
        for i in range(FIELDS):
            for p in range(start, start + SWEEPS):
                diagonal = inv[0, i, p]
                inv[coarse, i, p] = 1.0 / (diagonal - (fine_rate - coarse_rate) * masses[i])
                inv[0, i, p] = 1.0 / diagonal

    def hand_on(copies, wide_ref, slot):
        copies[0].wait_recv()
        for i in range(MASSIVE):
            for p in range(thick):
                passed_on[slot, i, thick - 1 - p] = wide_ref[i, first + p]
        copies[2].start()

    def add_w(start):
        for i in range(MASSIVE):
            span = pl.ds(start, SWEEPS)
            right[last, i, span] = right[last, i, span] + w_right[i, span]

    def begin(rhs, factor, start, stop):
        def body(p, carry):
            for i in range(FIELDS):
                xs[0, i, p] = rhs[i, p] * factor[i, p]
            return carry

        lax.fori_loop(start, stop, body, 0, unroll=True)

    def sweep(number, rhs, factor, start, stop, result=None):
        src = xs.at[number - 1]

        def body(p, carry):
            x = [src[i, p] for i in range(FIELDS)]
            for i in range(FIELDS):
                vertical = src[i, p - 1] + src[i, p + 1]
                total = rhs[i, p] + (operator_scale * fibre_weight * diffusion[i]) * vertical
                mixed = None
                for j in range(FIELDS):
                    if j != i:
                        term = (operator_scale * reaction[j][i]) * x[j]
                        mixed = term if mixed is None else mixed + term
                total = total + mixed
                along = jnp.where(row > 0, pltpu.roll(x[i], 1, 0), 0.0) + jnp.where(
                    row < 7, pltpu.roll(x[i], 7, 0), 0.0
                )
                across = jnp.where(col > 0, pltpu.roll(x[i], 1, 1), 0.0) + jnp.where(
                    col < 127, pltpu.roll(x[i], 127, 1), 0.0
                )
                total = total + (operator_scale * diffusion[i]) * (along + across)
                if result is None:
                    xs[number, i, p] = total * factor[i, p]
                else:
                    result[i, p - first] = total * factor[i, p]
            return carry

        lax.fori_loop(start, stop, body, 0, unroll=True)

    def solve(rhs, factor, result, near, far):
        begin(rhs, factor, first, end)
        sweep(1, rhs, factor, first + 1, end - 1)
        near()
        begin(rhs, factor, end, wide)
        for number in range(1, SWEEPS):
            start = end - 1 if number == 1 else first + number
            sweep(number, rhs, factor, start, wide - number)
        far()
        begin(rhs, factor, 0, first)
        for number in range(1, SWEEPS):
            sweep(number, rhs, factor, number, first + number)
        sweep(SWEEPS, rhs, factor, first, end, result)

    def wait_other(copies):
        pl.when(has_other)(copies[1].wait_recv)

    for n in range(last, -1, -1):
        if n == last:
            halo_start(inv_copies[n - 1])
            halo_start(rest_copies)

            @pl.when(has_next)
            def _():
                hand_on(w_copies, w_right, 0)

            add_w(first)
        elif n == last - 1:
            for m in range(n):
                halo_start(inv_copies[n - 1 - m])
        if n == 0:
            inv_copies[0][0].wait_recv()
            invert_first(end)

            @pl.when(has_other)
            def _():
                inv_copies[0][1].wait_recv()
                invert_first(0)

            @pl.when(t == tms - 1)
            def _():
                solve(rel_right, inv.at[coarse], zero_q, lambda: None, lambda: None)

        def near(n=n):
            if n > 0:
                inv_copies[n][0].wait_recv()
            if n == last - 1:
                rest_copies[0].wait_recv()
            right_copies[n][0].wait_recv()
            if n == last:
                pl.when(has_next)(w_copies[2].wait_recv)
                add_w(end)

        def far(n=n):
            if n > 0:
                wait_other(inv_copies[n])
            if n == last - 1:
                wait_other(rest_copies)
            wait_other(right_copies[n])
            if n == last:
                pl.when(jnp.logical_and(has_next, has_other))(w_copies[1].wait_recv)
                add_w(0)

        solve(right.at[n], inv.at[n], adj.at[n], near, far)
        if n == last:
            pl.when(has_next)(z_g.wait_recv)
        if n > 0:
            for i in range(MASSIVE):
                for p in range(thick):
                    before = g_got[i, p] if n == last else adj[n + 1, i, p]
                    value = source_ref[n - 1, i, place[p]] + (4.0 * adj[n, i, p] - before)
                    right[n - 1, i, first + p] = value
                    right_turned[n - 1, i, thick - 1 - p] = value
            halo_start(right_copies[n - 1])
        else:
            for i in range(MASSIVE):
                for p in range(thick):
                    value = adj[0, i, p] - 0.25 * adj[1, i, p]
                    rel_src[i, p] = value
                    rel_turned[i, thick - 1 - p] = value
            spread_start(rel_copies)

    def send_corrected():
        for i in range(MASSIVE):
            for p in range(thick):
                value = cor[0, i, p] - 0.25 * cor[1, i, p]
                cor_src[i, p] = value
                cor_turned[i, thick - 1 - p] = value
        spread_start(cor_copies)
        for i in range(FIELDS):
            change[i] = cor[0, i] - adj[0, i]
        pl.when(has_prev)(z_change.start)

    @pl.when(t == tms - 1)
    def _():
        for i in range(FIELDS):
            zero_p1 = 0.5 * (zero_q[i] + 0.0)
            cor[0, i] = zero_q[i] + (adj[0, i] - zero_q[i])
            cor[1, i] = zero_p1 + (adj[1, i] - zero_p1)
        send_corrected()

    for n in range(last, -1, -1):
        for i in range(FIELDS):
            for p in range(thick):
                term = adj[n, i, p] * states_ref[n, i, place[p]].astype(jnp.float32)
                spot = i * thick + p
                part[spot] = term if n == last else part[spot] + term

    chunk = FIELDS * thick // tms
    grad_one, grad_two, grad_in = [], [], []
    for hop in range(1, tms):
        target = lax.rem(t + hop, tms)
        origin = lax.rem(t + tms - hop, tms)
        grad_one.append(
            pltpu.make_async_remote_copy(
                part.at[pl.ds(target * chunk, chunk)], part_got.at[hop - 1],
                grad_send.at[0, hop - 1], grad_recv.at[0, hop - 1],
                device_id={"tm": target}, device_id_type=MESH,
            )
        )
        mine = whole.at[pl.ds(t * chunk, chunk)]
        grad_two.append(
            pltpu.make_async_remote_copy(
                mine, mine, grad_send.at[1, hop - 1], grad_recv.at[1, hop - 1],
                device_id={"tm": target}, device_id_type=MESH,
            )
        )
        theirs = whole.at[pl.ds(origin * chunk, chunk)]
        grad_in.append(
            pltpu.make_async_remote_copy(
                theirs, theirs, grad_send.at[1, hop - 1], grad_recv.at[1, hop - 1],
                device_id={"tm": target}, device_id_type=MESH,
            )
        )
    for copy in grad_one:
        copy.start()

    @pl.when(has_next)
    def _():
        hand_on(rel_copies, rel_right, 1)

        @pl.when(t == tms - 2)
        def _():
            hand_on(cor_copies, cor_right, 2)

        def far():
            pl.when(has_other)(rel_copies[1].wait_recv)

        solve(rel_right, inv.at[coarse], rel_q, rel_copies[2].wait_recv, far)
        for i in range(FIELDS):
            offs[0, i] = adj[0, i] - rel_q[i]
            offs[1, i] = adj[1, i] - 0.5 * rel_q[i]

    def share_gradient():
        for copy in grad_one:
            copy.wait_recv()
        total = part[pl.ds(t * chunk, chunk)]
        for hop in range(1, tms):
            total = total + part_got[hop - 1]
        whole[pl.ds(t * chunk, chunk)] = time_step * total
        for copy in grad_two:
            copy.start()

    pl.when(jnp.logical_or(t < tms - 2, t == tms - 1))(share_gradient)

    @pl.when(has_next)
    def _():
        @pl.when(t < tms - 2)
        def _():
            hand_on(cor_copies, cor_right, 2)

        def far():
            pl.when(has_other)(cor_copies[1].wait_recv)

        solve(cor_right, inv.at[coarse], cor_q, cor_copies[2].wait_recv, far)
        z_change.wait_recv()
        for i in range(FIELDS):
            cor[0, i] = cor_q[i] + offs[0, i]
            cor[1, i] = 0.5 * (cor_q[i] + change_got[i]) + offs[1, i]
        send_corrected()

    pl.when(t == tms - 2)(share_gradient)

    for pair in range(2):
        for i in range(FIELDS):
            for p in range(thick):
                corrected_ref[0, pair, i, place[p]] = cor[pair, i, p]
    for copy in grad_in:
        copy.wait_recv()
    for i in range(FIELDS):
        for p in range(thick):
            gradient_ref[i, place[p]] = whole[i * thick + p]

    halos = inv_copies + right_copies + [rest_copies]
    for copies in halos:
        copies[0].wait_send()

    @pl.when(has_other)
    def _():
        for copies in halos:
            copies[1].wait_send()

    @pl.when(has_next)
    def _():
        for copies in (w_copies, rel_copies, cor_copies):
            copies[2].wait_send()

    @pl.when(has_prev)
    def _():
        for copies in (w_copies, rel_copies, cor_copies):
            copies[0].wait_send()
            pl.when(has_other)(copies[1].wait_send)
        for copy in (z_g, z_change):
            copy.wait_send()

    for copy in grad_one + grad_two:
        copy.wait_send()


def on_device(tms, spaces, forward_states, adjoint_source, source_gain, guess_pairs):
    steps, _, thick = forward_states.shape[:3]
    wide = thick + 2 * SWEEPS
    vmem = lambda *shape: pltpu.VMEM(shape + (8, 128), jnp.float32)
    chunk = FIELDS * thick // tms
    in_vmem = pl.BlockSpec(memory_space=pltpu.VMEM)
    heavy = vmem(MASSIVE, thick)
    every = vmem(FIELDS, thick)
    return pl.pallas_call(
        functools.partial(kernel, steps, thick, tms, spaces),
        out_shape=(
            jax.ShapeDtypeStruct(guess_pairs.shape, jnp.float32),
            jax.ShapeDtypeStruct(source_gain.shape, jnp.float32),
        ),
        in_specs=[pl.BlockSpec(memory_space=pltpu.HBM)] * 4,
        out_specs=(in_vmem, in_vmem),
        scratch_shapes=[
            pltpu.VMEM(forward_states.shape, forward_states.dtype),
            pltpu.VMEM(adjoint_source.shape, jnp.float32),
            pltpu.VMEM(source_gain.shape, jnp.float32),
            pltpu.VMEM(guess_pairs.shape, jnp.float32),
            vmem(steps + 1, FIELDS, wide),
            vmem(steps, FIELDS, thick),
            vmem(steps, FIELDS, wide),
            vmem(steps, FIELDS, thick),
            vmem(MASSIVE, wide),
            vmem(FIELDS, wide),
            vmem(FIELDS, wide),
            vmem(SWEEPS, FIELDS, wide),
            vmem(steps, FIELDS, thick),
            every,
            every,
            every,
            vmem(2, FIELDS, thick),
            vmem(2, FIELDS, thick),
            heavy,
            heavy,
            heavy,
            heavy,
            heavy,
            heavy,
            heavy,
            heavy,
            every,
            every,
            vmem(3, MASSIVE, thick),
            vmem(FIELDS * thick),
            vmem(tms - 1, chunk),
            vmem(FIELDS * thick),
            pltpu.SemaphoreType.DMA((4,)),
            pltpu.SemaphoreType.DMA((2 * steps + 5, 2)),
            pltpu.SemaphoreType.DMA((2 * steps + 5, 2)),
            pltpu.SemaphoreType.DMA((8,)),
            pltpu.SemaphoreType.DMA((8,)),
            pltpu.SemaphoreType.DMA((2, tms - 1)),
            pltpu.SemaphoreType.DMA((2, tms - 1)),
        ],
        compiler_params=pltpu.CompilerParams(
            collective_id=0, has_side_effects=True, vmem_limit_bytes=64 * 1024 * 1024
        ),
        name="adjoint_cycle",
    )(forward_states, adjoint_source, source_gain, guess_pairs)


def solution(mesh):
    placed = (
        P("tm", None, "space", None, None),
        P("tm", None, "space", None, None),
        P(None, "space", None, None),
        P("tm", None, None, "space", None, None),
    )
    return jax.shard_map(
        functools.partial(on_device, mesh.shape["tm"], mesh.shape["space"]),
        mesh=mesh,
        in_specs=placed,
        out_specs=(P("tm", None, None, "space", None, None), P(None, "space", None, None)),
        check_vma=False,
    )
```

```python
import functools

import jax
import jax.numpy as jnp
from jax import lax
from jax.experimental import pallas as pl
from jax.experimental.pallas import tpu as pltpu
from jax.sharding import PartitionSpec as P

SWEEPS = 4
FIELDS = 4
MASSIVE = 3

diffusion = (2.4, 1.2, 0.6, 4.0)
fibre_weight = 128.0
reaction = (
    (-14.4, 7.2, -4.8, 2.4),
    (4.8, -19.2, 7.2, -4.8),
    (-7.2, 2.4, -12.0, 7.2),
    (4.8, -7.2, 2.4, -38.4),
)
self_rates = (-14.4, -19.2, -12.0, -38.4)
masses = (1.0, 1.0, 1.0, 0.0)
fine_rate = 3.0
coarse_rate = 0.75
time_step = 0.5
operator_scale = 0.0078125
state_weight = 0.1
gain_weight = 0.25

MESH = pl.DeviceIdType.MESH


def kernel(
    steps, thick, tms, spaces,
    states_hbm, source_hbm, gain_hbm, guess_hbm,
    corrected_ref, gradient_ref,
    states_ref, source_ref, gain_ref, guess_ref,
    inv, inv_turned, right, right_turned, w_right, rel_right, cor_right, xs,
    adj, zero_q, rel_q, cor_q, offs, cor,
    w_src, w_turned, g_src, g_got, rel_src, rel_turned, cor_src, cor_turned, change, change_got,
    passed_on, part, part_got, whole,
    load_sem, halo_send, halo_recv, z_send, z_recv, grad_send, grad_recv,
):
    t = lax.axis_index("tm")
    s = lax.axis_index("space")
    odd = lax.rem(s, 2)
    sibling = s + 1 - 2 * odd
    other = s - 1 + 2 * odd
    has_other = jnp.logical_and(other >= 0, other < spaces)
    has_next, has_prev = t < tms - 1, t > 0
    wide = thick + 2 * SWEEPS
    first, end = SWEEPS, SWEEPS + thick
    own = pl.ds(SWEEPS, thick)
    low = pl.ds(0, SWEEPS)
    high = pl.ds(SWEEPS + thick, SWEEPS)
    heavy = pl.ds(0, MASSIVE)
    coarse = steps
    last = steps - 1
    row = lax.broadcasted_iota(jnp.int32, (8, 128), 0)
    col = lax.broadcasted_iota(jnp.int32, (8, 128), 1)
    place = [p + odd * (thick - 1 - 2 * p) for p in range(thick)]

    loads = [
        pltpu.make_async_copy(hbm, ref, load_sem.at[k])
        for k, (hbm, ref) in enumerate(
            (
                (guess_hbm, guess_ref),
                (states_hbm, states_ref),
                (gain_hbm, gain_ref),
                (source_hbm, source_ref),
            )
        )
    ]
    for load in loads:
        load.start()

    def to_sibling(index, src, dst):
        return pltpu.make_async_remote_copy(
            src, dst, halo_send.at[index, 0], halo_recv.at[index, 0],
            device_id={"space": sibling}, device_id_type=MESH,
        )

    def halo_copies(index, src, view):
        off = pltpu.make_async_remote_copy(
            src, view(low), halo_send.at[index, 1], halo_recv.at[index, 1],
            device_id={"space": other}, device_id_type=MESH,
        )
        return to_sibling(index, src, view(high)), off

    def halo_start(copies):
        pl.when(has_other)(copies[1].start)
        copies[0].start()

    def to_previous(index, src, dst):
        return pltpu.make_async_remote_copy(
            src, dst, z_send.at[index], z_recv.at[index],
            device_id={"tm": t - 1}, device_id_type=MESH,
        )

    def spread_copies(index, halo_index, src, turned, wide_ref):
        straight = to_previous(index, src, wide_ref.at[heavy, own])
        across = pltpu.make_async_remote_copy(
            turned, wide_ref.at[heavy, low], z_send.at[index + 1], z_recv.at[index + 1],
            device_id={"tm": t - 1, "space": other}, device_id_type=MESH,
        )
        onward = to_sibling(halo_index, passed_on.at[index // 2], wide_ref.at[heavy, high])
        return straight, across, onward

    inv_copies = [
        halo_copies(n, inv_turned.at[n], lambda p, n=n: inv.at[n, :, p])
        for n in range(steps)
    ]
    right_copies = [
        halo_copies(steps + 1 + n, right_turned.at[n], lambda p, n=n: right.at[n, :, p])
        if n == last
        else halo_copies(
            steps + 1 + n, right_turned.at[n, heavy], lambda p, n=n: right.at[n, heavy, p]
        )
        for n in range(steps)
    ]
    rest_copies = halo_copies(
        2 * steps + 1,
        right_turned.at[pl.ds(0, last), MASSIVE],
        lambda p: right.at[pl.ds(0, last), MASSIVE, p],
    )
    w_copies = spread_copies(0, 2 * steps + 2, w_src, w_turned, w_right)
    rel_copies = spread_copies(2, 2 * steps + 3, rel_src, rel_turned, rel_right)
    cor_copies = spread_copies(4, 2 * steps + 4, cor_src, cor_turned, cor_right)
    z_g = to_previous(6, g_src, g_got)
    z_change = to_previous(7, change, change_got)

    rel_right[...] = jnp.zeros_like(rel_right)
    cor_right[...] = jnp.zeros_like(cor_right)

    @pl.when(jnp.logical_not(has_other))
    def _():
        inv[:, :, low] = jnp.zeros((steps + 1, FIELDS, SWEEPS, 8, 128), jnp.float32)
        right[:, :, low] = jnp.zeros((steps, FIELDS, SWEEPS, 8, 128), jnp.float32)
        w_right[:, low] = jnp.zeros((MASSIVE, SWEEPS, 8, 128), jnp.float32)

    @pl.when(t == tms - 1)
    def _():
        w_right[...] = jnp.zeros_like(w_right)
        g_got[...] = jnp.zeros_like(g_got)

    barrier = pltpu.get_barrier_semaphore()

    def greet(**device):
        pl.semaphore_signal(barrier, inc=1, device_id=device, device_id_type=MESH)

    for hop in range(1, tms):
        greet(tm=lax.rem(t + hop, tms))
    greet(space=sibling)

    @pl.when(has_other)
    def _():
        greet(space=other)
        pl.when(has_next)(lambda: greet(tm=t + 1, space=other))
        pl.when(has_prev)(lambda: greet(tm=t - 1, space=other))

    def fill_inverse(slot, n, rate):
        for i in range(FIELDS):
            base = rate * masses[i] + operator_scale * (
                (2.0 * fibre_weight + 4.0) * diffusion[i] - self_rates[i]
            )
            for p in range(thick):
                u = states_ref[n, i, place[p]].astype(jnp.float32)
                diagonal = base + state_weight * u * u - gain_weight * gain_ref[i, place[p]]
                value = 1.0 / diagonal
                inv[slot, i, first + p] = value
                if slot < steps:
                    inv_turned[slot, i, thick - 1 - p] = diagonal if slot == 0 else value

    loads[0].wait()
    for i in range(MASSIVE):
        for p in range(thick):
            one = guess_ref[0, 0, i, place[p]]
            value = 4.0 * one - guess_ref[0, 1, i, place[p]]
            w_src[i, p] = value
            w_turned[i, thick - 1 - p] = value
            g_src[i, p] = one
    loads[1].wait()
    loads[2].wait()
    fill_inverse(last, last, fine_rate)
    loads[3].wait()
    for i in range(FIELDS):
        for p in range(thick):
            for n in [last] if i < MASSIVE else range(steps):
                value = source_ref[n, i, place[p]]
                right[n, i, first + p] = value
                right_turned[n, i, thick - 1 - p] = value

    both = has_next.astype(jnp.int32) + has_prev.astype(jnp.int32)
    pl.semaphore_wait(barrier, tms + has_other.astype(jnp.int32) * (1 + both))

    def spread_start(copies):
        @pl.when(has_prev)
        def _():
            copies[0].start()
            pl.when(has_other)(copies[1].start)

    spread_start(w_copies)
    halo_start(inv_copies[last])
    halo_start(right_copies[last])
    pl.when(has_prev)(z_g.start)
    for n in range(last):
        fill_inverse(n, n, fine_rate)
    fill_inverse(coarse, 0, coarse_rate)

    def invert_first(start):
        for i in range(FIELDS):
            for p in range(start, start + SWEEPS):
                diagonal = inv[0, i, p]
                inv[coarse, i, p] = 1.0 / (diagonal - (fine_rate - coarse_rate) * masses[i])
                inv[0, i, p] = 1.0 / diagonal

    def hand_on(copies, wide_ref, slot):
        copies[0].wait_recv()
        for i in range(MASSIVE):
            for p in range(thick):
                passed_on[slot, i, thick - 1 - p] = wide_ref[i, first + p]
        copies[2].start()

    def add_w(start):
        for i in range(MASSIVE):
            span = pl.ds(start, SWEEPS)
            right[last, i, span] = right[last, i, span] + w_right[i, span]

    def begin(rhs, factor, start, stop):
        def body(p, carry):
            for i in range(FIELDS):
                xs[0, i, p] = rhs[i, p] * factor[i, p]
            return carry

        lax.fori_loop(start, stop, body, 0, unroll=True)

    def sweep(number, rhs, factor, start, stop, result=None):
        src = xs.at[number - 1]

        def body(p, carry):
            x = [src[i, p] for i in range(FIELDS)]
            for i in range(FIELDS):
                vertical = src[i, p - 1] + src[i, p + 1]
                total = rhs[i, p] + (operator_scale * fibre_weight * diffusion[i]) * vertical
                mixed = None
                for j in range(FIELDS):
                    if j != i:
                        term = (operator_scale * reaction[j][i]) * x[j]
                        mixed = term if mixed is None else mixed + term
                total = total + mixed
                along = jnp.where(row > 0, pltpu.roll(x[i], 1, 0), 0.0) + jnp.where(
                    row < 7, pltpu.roll(x[i], 7, 0), 0.0
                )
                across = jnp.where(col > 0, pltpu.roll(x[i], 1, 1), 0.0) + jnp.where(
                    col < 127, pltpu.roll(x[i], 127, 1), 0.0
                )
                total = total + (operator_scale * diffusion[i]) * (along + across)
                if result is None:
                    xs[number, i, p] = total * factor[i, p]
                else:
                    result[i, p - first] = total * factor[i, p]
            return carry

        lax.fori_loop(start, stop, body, 0, unroll=True)

    def solve(rhs, factor, result, near, far):
        begin(rhs, factor, first, end)
        sweep(1, rhs, factor, first + 1, end - 1)
        near()
        begin(rhs, factor, end, wide)
        for number in range(1, SWEEPS):
            start = end - 1 if number == 1 else first + number
            sweep(number, rhs, factor, start, wide - number)
        far()
        begin(rhs, factor, 0, first)
        for number in range(1, SWEEPS):
            sweep(number, rhs, factor, number, first + number)
        sweep(SWEEPS, rhs, factor, first, end, result)

    def wait_other(copies):
        pl.when(has_other)(copies[1].wait_recv)

    for n in range(last, -1, -1):
        if n == last:
            halo_start(inv_copies[n - 1])
            halo_start(rest_copies)

            @pl.when(has_next)
            def _():
                hand_on(w_copies, w_right, 0)

            add_w(first)
        elif n == last - 1:
            for m in range(n):
                halo_start(inv_copies[n - 1 - m])
        if n == 0:
            inv_copies[0][0].wait_recv()
            invert_first(end)

            @pl.when(has_other)
            def _():
                inv_copies[0][1].wait_recv()
                invert_first(0)

            @pl.when(t == tms - 1)
            def _():
                solve(rel_right, inv.at[coarse], zero_q, lambda: None, lambda: None)

        def near(n=n):
            if n > 0:
                inv_copies[n][0].wait_recv()
            if n == last - 1:
                rest_copies[0].wait_recv()
            right_copies[n][0].wait_recv()
            if n == last:
                pl.when(has_next)(w_copies[2].wait_recv)
                add_w(end)

        def far(n=n):
            if n > 0:
                wait_other(inv_copies[n])
            if n == last - 1:
                wait_other(rest_copies)
            wait_other(right_copies[n])
            if n == last:
                pl.when(jnp.logical_and(has_next, has_other))(w_copies[1].wait_recv)
                add_w(0)

        solve(right.at[n], inv.at[n], adj.at[n], near, far)
        if n == last:
            pl.when(has_next)(z_g.wait_recv)
        if n > 0:
            for i in range(MASSIVE):
                for p in range(thick):
                    before = g_got[i, p] if n == last else adj[n + 1, i, p]
                    value = source_ref[n - 1, i, place[p]] + (4.0 * adj[n, i, p] - before)
                    right[n - 1, i, first + p] = value
                    right_turned[n - 1, i, thick - 1 - p] = value
            halo_start(right_copies[n - 1])
        else:
            for i in range(MASSIVE):
                for p in range(thick):
                    value = adj[0, i, p] - 0.25 * adj[1, i, p]
                    rel_src[i, p] = value
                    rel_turned[i, thick - 1 - p] = value
            spread_start(rel_copies)

    def send_corrected():
        for i in range(MASSIVE):
            for p in range(thick):
                value = cor[0, i, p] - 0.25 * cor[1, i, p]
                cor_src[i, p] = value
                cor_turned[i, thick - 1 - p] = value
        spread_start(cor_copies)
        for i in range(FIELDS):
            change[i] = cor[0, i] - adj[0, i]
        pl.when(has_prev)(z_change.start)

    @pl.when(t == tms - 1)
    def _():
        for i in range(FIELDS):
            zero_p1 = 0.5 * (zero_q[i] + 0.0)
            cor[0, i] = zero_q[i] + (adj[0, i] - zero_q[i])
            cor[1, i] = zero_p1 + (adj[1, i] - zero_p1)
        send_corrected()

    for n in range(last, -1, -1):
        for i in range(FIELDS):
            for p in range(thick):
                term = adj[n, i, p] * states_ref[n, i, place[p]].astype(jnp.float32)
                spot = i * thick + p
                part[spot] = term if n == last else part[spot] + term

    chunk = FIELDS * thick // tms
    grad_one, grad_two, grad_in = [], [], []
    for hop in range(1, tms):
        target = lax.rem(t + hop, tms)
        origin = lax.rem(t + tms - hop, tms)
        grad_one.append(
            pltpu.make_async_remote_copy(
                part.at[pl.ds(target * chunk, chunk)], part_got.at[hop - 1],
                grad_send.at[0, hop - 1], grad_recv.at[0, hop - 1],
                device_id={"tm": target}, device_id_type=MESH,
            )
        )
        mine = whole.at[pl.ds(t * chunk, chunk)]
        grad_two.append(
            pltpu.make_async_remote_copy(
                mine, mine, grad_send.at[1, hop - 1], grad_recv.at[1, hop - 1],
                device_id={"tm": target}, device_id_type=MESH,
            )
        )
        theirs = whole.at[pl.ds(origin * chunk, chunk)]
        grad_in.append(
            pltpu.make_async_remote_copy(
                theirs, theirs, grad_send.at[1, hop - 1], grad_recv.at[1, hop - 1],
                device_id={"tm": target}, device_id_type=MESH,
            )
        )
    for copy in grad_one:
        copy.start()

    @pl.when(has_next)
    def _():
        hand_on(rel_copies, rel_right, 1)

        @pl.when(t == tms - 2)
        def _():
            hand_on(cor_copies, cor_right, 2)

        def far():
            pl.when(has_other)(rel_copies[1].wait_recv)

        solve(rel_right, inv.at[coarse], rel_q, rel_copies[2].wait_recv, far)
        for i in range(FIELDS):
            offs[0, i] = adj[0, i] - rel_q[i]
            offs[1, i] = adj[1, i] - 0.5 * rel_q[i]

    def share_gradient():
        for copy in grad_one:
            copy.wait_recv()
        total = part[pl.ds(t * chunk, chunk)]
        for hop in range(1, tms):
            total = total + part_got[hop - 1]
        whole[pl.ds(t * chunk, chunk)] = total
        for copy in grad_two:
            copy.start()

    pl.when(jnp.logical_or(t < tms - 2, t == tms - 1))(share_gradient)

    @pl.when(has_next)
    def _():
        @pl.when(t < tms - 2)
        def _():
            hand_on(cor_copies, cor_right, 2)

        def far():
            pl.when(has_other)(cor_copies[1].wait_recv)

        solve(cor_right, inv.at[coarse], cor_q, cor_copies[2].wait_recv, far)
        z_change.wait_recv()
        for i in range(FIELDS):
            cor[0, i] = cor_q[i] + offs[0, i]
            cor[1, i] = 0.5 * (cor_q[i] + change_got[i]) + offs[1, i]
        send_corrected()

    pl.when(t == tms - 2)(share_gradient)

    for pair in range(2):
        for i in range(FIELDS):
            for p in range(thick):
                corrected_ref[0, pair, i, place[p]] = cor[pair, i, p]
    for copy in grad_in:
        copy.wait_recv()
    for i in range(FIELDS):
        for p in range(thick):
            gradient_ref[i, place[p]] = whole[i * thick + p]

    halos = inv_copies + right_copies + [rest_copies]
    for copies in halos:
        copies[0].wait_send()

    @pl.when(has_other)
    def _():
        for copies in halos:
            copies[1].wait_send()

    @pl.when(has_next)
    def _():
        for copies in (w_copies, rel_copies, cor_copies):
            copies[2].wait_send()

    @pl.when(has_prev)
    def _():
        for copies in (w_copies, rel_copies, cor_copies):
            copies[0].wait_send()
            pl.when(has_other)(copies[1].wait_send)
        for copy in (z_g, z_change):
            copy.wait_send()

    for copy in grad_one + grad_two:
        copy.wait_send()


def on_device(tms, spaces, forward_states, adjoint_source, source_gain, guess_pairs):
    steps, _, thick = forward_states.shape[:3]
    wide = thick + 2 * SWEEPS
    vmem = lambda *shape: pltpu.VMEM(shape + (8, 128), jnp.float32)
    chunk = FIELDS * thick // tms
    in_vmem = pl.BlockSpec(memory_space=pltpu.VMEM)
    heavy = vmem(MASSIVE, thick)
    every = vmem(FIELDS, thick)
    corrected, summed = pl.pallas_call(
        functools.partial(kernel, steps, thick, tms, spaces),
        out_shape=(
            jax.ShapeDtypeStruct(guess_pairs.shape, jnp.float32),
            jax.ShapeDtypeStruct(source_gain.shape, jnp.float32),
        ),
        in_specs=[pl.BlockSpec(memory_space=pltpu.HBM)] * 4,
        out_specs=(in_vmem, in_vmem),
        scratch_shapes=[
            pltpu.VMEM(forward_states.shape, forward_states.dtype),
            pltpu.VMEM(adjoint_source.shape, jnp.float32),
            pltpu.VMEM(source_gain.shape, jnp.float32),
            pltpu.VMEM(guess_pairs.shape, jnp.float32),
            vmem(steps + 1, FIELDS, wide),
            vmem(steps, FIELDS, thick),
            vmem(steps, FIELDS, wide),
            vmem(steps, FIELDS, thick),
            vmem(MASSIVE, wide),
            vmem(FIELDS, wide),
            vmem(FIELDS, wide),
            vmem(SWEEPS, FIELDS, wide),
            vmem(steps, FIELDS, thick),
            every,
            every,
            every,
            vmem(2, FIELDS, thick),
            vmem(2, FIELDS, thick),
            heavy,
            heavy,
            heavy,
            heavy,
            heavy,
            heavy,
            heavy,
            heavy,
            every,
            every,
            vmem(3, MASSIVE, thick),
            vmem(FIELDS * thick),
            vmem(tms - 1, chunk),
            vmem(FIELDS * thick),
            pltpu.SemaphoreType.DMA((4,)),
            pltpu.SemaphoreType.DMA((2 * steps + 5, 2)),
            pltpu.SemaphoreType.DMA((2 * steps + 5, 2)),
            pltpu.SemaphoreType.DMA((8,)),
            pltpu.SemaphoreType.DMA((8,)),
            pltpu.SemaphoreType.DMA((2, tms - 1)),
            pltpu.SemaphoreType.DMA((2, tms - 1)),
        ],
        compiler_params=pltpu.CompilerParams(
            collective_id=0, has_side_effects=True, vmem_limit_bytes=64 * 1024 * 1024
        ),
        name="adjoint_cycle",
    )(forward_states, adjoint_source, source_gain, guess_pairs)
    return corrected, time_step * summed


def solution(mesh):
    placed = (
        P("tm", None, "space", None, None),
        P("tm", None, "space", None, None),
        P(None, "space", None, None),
        P("tm", None, None, "space", None, None),
    )
    return jax.shard_map(
        functools.partial(on_device, mesh.shape["tm"], mesh.shape["space"]),
        mesh=mesh,
        in_specs=placed,
        out_specs=(P("tm", None, None, "space", None, None), P(None, "space", None, None)),
        check_vma=False,
    )
```
